128 devices in a mesh: range: 4 (over z_hi, core), azimuth: 32 (over x, y, z_lo).
Axes of the slice: x: 4, y: 4, z: 4 (z_hi: 2, z_lo: 2; z = z_hi * 2 + z_lo), core: 2. Of those that a mesh axis runs over, the one named last changes fastest.
Arguments:
- features: bfloat16 [4, 64, 64, 4096], P(None, None, 'range', 'azimuth'), may hold values from -6 to 6
- state_init: bfloat16 [64, 64, 4096], P(None, 'range', 'azimuth'), may hold values from -3 to 3
- kernel: float32 [64, 3, 3], replicated, may hold values from -2 to 2
- gate_weight: bfloat16 [128, 128], replicated, may hold values from -0.5 to 0.5
- cand_weight: bfloat16 [64, 64], replicated, may hold values from -0.75 to 0.75
- recur_weight: bfloat16 [64, 64], replicated, may hold values from -0.75 to 0.75
- down_weight: bfloat16 [128, 1024], replicated, may hold values from -0.1875 to 0.1875
- owner_map: int32 [4, 32, 4], P('range', 'azimuth'), may hold values from 0 to 3, as said below
- dest_map: int32 [4, 32, 4], P('range', 'azimuth'), may hold values from 0 to 3
- cart_cot: bfloat16 [4, 32, 4, 128, 128], P('range', 'azimuth'), may hold values from -6 to 6
Outputs:
- cart: float32 [4, 32, 4, 128, 128], P('range', 'azimuth')
- grad_features: bfloat16 [4, 64, 64, 4096], P(None, None, 'range', 'azimuth')
- grad_state: float32 [64, 64, 4096], P(None, 'range', 'azimuth')
- grad_kernel: float32 [64, 3, 3], replicated
- grad_gate: float32 [128, 128], replicated
- grad_cand: float32 [64, 64], replicated
- grad_recur: float32 [64, 64], replicated
- grad_down: float32 [128, 1024], replicated
The draws below stay inside these ranges and needn't reach their ends.
Inputs may be any that keep to these rules, and one draw needn't show every extreme that they name: `owner_map`: no tile sends more than 2 of its 4 blocks to one owner; in every azimuth column one owner receives exactly 2 blocks from every tile of the column.
All inputs are finite; a program needn't handle non-finite values.
Results may differ from the reference program's by a relative error of at most 0.0065.
Values may be sent and summed in bfloat16 or wider, within the bound.
A program may use at most 128 MiB of HBM per device.

```python
import math
import jax
import jax.numpy as jnp
from jax import lax

CHANNELS = 64
COARSE = 128
SLICES = 4
DILATION = 8
BLOCK = 128
RANGE_DEV = 16
AZIM_DEV = 128
RANGE_CELLS = 64
AZIM_CELLS = 4096
BLOCKS_SLICE = 1
BLOCKS = 4
CAPACITY = 2
N_RANGE = 4
N_AZIMUTH = 32


def draw_owner_map(key, part):
    key_full = jax.random.fold_in(key, 11)
    key_rank = jax.random.fold_in(key, 12)
    key_turn = jax.random.fold_in(key, 13)
    full_owner = jax.random.randint(key_full, (1, N_AZIMUTH, 1), 0, N_RANGE).astype(jnp.int32)
    scores = jax.random.randint(key_rank, (N_RANGE, N_AZIMUTH, BLOCKS), 0, 1 << 20).astype(jnp.int32) * BLOCKS + jnp.arange(BLOCKS, dtype=jnp.int32)[None, None, :]
    ranked = jnp.argsort(jnp.argsort(scores, axis=2), axis=2).astype(jnp.int32)
    turned = jax.random.randint(key_turn, (N_RANGE, N_AZIMUTH, 1), 0, N_RANGE - 1).astype(jnp.int32)
    others = (full_owner + 1 + (ranked - CAPACITY + turned) % (N_RANGE - 1)) % N_RANGE
    return jnp.where(ranked < CAPACITY, full_owner, others).astype(jnp.int32)


def touch_ends(array, stream_key, least, largest):
    shape = array.shape
    place = [jax.random.randint(jax.random.fold_in(stream_key, axis), (), 0, shape[axis]) for axis in range(len(shape))]
    array = array.at[tuple(place)].set(least)
    longest = shape.index(max(shape))
    place[longest] = (place[longest] + 1) % shape[longest]
    return array.at[tuple(place)].set(largest)


def steps_of(key, extent, pieces, smallest, top_value):
    def one(position, blocks):
        draws = jax.random.uniform(jax.random.fold_in(jax.random.fold_in(key, 6), position), (blocks,), jnp.float32, smallest / len(pieces), top_value / len(pieces))
        return jnp.repeat(jnp.exp(draws), extent[position] // blocks).reshape((-1,) + (1,) * (len(extent) - position - 1))

    factor_of = one(*pieces[0])
    for cut in pieces[1:]:
        factor_of = factor_of * one(*cut)
    return factor_of


def centred(own_key, shape, spread, limit, shards=(), kind=jnp.bfloat16):
    drawn = spread * jax.random.normal(own_key, shape, jnp.float32)
    if shards:
        drawn = drawn * steps_of(own_key, shape, shards, -0.22, 0.18)
    return jnp.clip(drawn, -limit, limit).astype(kind)


def setup_inputs(seed: int = 0) -> dict:
    key_of = jax.random.split(jax.random.key(seed), 11)
    features = centred(key_of[0], (SLICES, CHANNELS, RANGE_CELLS, AZIM_CELLS), 1.0, 6.0, ((2, 4), (3, 32)))
    state_init = centred(key_of[1], (CHANNELS, RANGE_CELLS, AZIM_CELLS), 0.5, 3.0, ((1, 4), (2, 32)))
    kernel = centred(key_of[2], (CHANNELS, 3, 3), 9 ** -0.5, 2.0, (), jnp.float32)
    gate_weight = centred(key_of[3], (2 * CHANNELS, 2 * CHANNELS), (2 * CHANNELS) ** -0.5, 0.5)
    cand_weight = centred(key_of[4], (CHANNELS, CHANNELS), CHANNELS ** -0.5, 0.75)
    recur_weight = centred(key_of[5], (CHANNELS, CHANNELS), CHANNELS ** -0.5, 0.75)
    down_weight = centred(key_of[6], (COARSE, 16 * CHANNELS), (16 * CHANNELS) ** -0.5, 0.1875)
    owner_map = draw_owner_map(jax.random.fold_in(key_of[10], 71), 0)
    dest_map = touch_ends(jax.random.randint(key_of[8], (N_RANGE, N_AZIMUTH, BLOCKS), 0, BLOCKS), jax.random.fold_in(key_of[8], 1), 0, BLOCKS - 1).astype(jnp.int32)
    cart_cot = centred(key_of[9], (N_RANGE, N_AZIMUTH, BLOCKS, COARSE, BLOCK), 1.0, 6.0, ((0, 4), (1, 32)))
    return dict(features=features, state_init=state_init, kernel=kernel, gate_weight=gate_weight, cand_weight=cand_weight, recur_weight=recur_weight, down_weight=down_weight, owner_map=owner_map, dest_map=dest_map, cart_cot=cart_cot)


def framed(field):
    taller = jnp.pad(field, ((0, 0), (1, 1), (0, 0)))
    return jnp.concatenate([taller[:, :, -DILATION:], taller, taller[:, :, :DILATION]], axis=2)

def depthwise(padded, kernel, tile_rows, tile_cols):
    summed = jnp.zeros((padded.shape[0], tile_rows, tile_cols), jnp.float32)
    for tap_row in range(3):
        for tap_col in range(3):
            window = padded[:, tap_row:tap_row + tile_rows, tap_col * DILATION:tap_col * DILATION + tile_cols]
            summed = summed + kernel[:, tap_row, tap_col][:, None, None] * window.astype(jnp.float32)
    return summed

def kernel_terms(padded, dconv, tile_rows, tile_cols):
    grads = dconv.astype(jnp.float32)
    outer_rows = []
    for tap_row in range(3):
        inner_cols = []
        for tap_col in range(3):
            window = padded[:, tap_row:tap_row + tile_rows, tap_col * DILATION:tap_col * DILATION + tile_cols]
            inner_cols.append(lax.optimization_barrier(jnp.sum(grads * window.astype(jnp.float32), axis=(1, 2))))
        outer_rows.append(jnp.stack(inner_cols, axis=1))
    return jnp.stack(outer_rows, axis=1)

def patches(values, tile_rows, tile_cols):
    channels = values.shape[0]
    shaped = values.reshape(channels, tile_rows // 4, 4, tile_cols // 4, 4).transpose(0, 2, 4, 1, 3)
    return shaped.reshape(16 * channels, tile_rows * tile_cols // 16)

def unpatches(grads, tile_rows, tile_cols):
    channels = grads.shape[0] // 16
    shaped = grads.reshape(channels, 4, 4, tile_rows // 4, tile_cols // 4).transpose(0, 3, 1, 4, 2)
    return shaped.reshape(channels, tile_rows * tile_cols)

def cross_cells(left, right):
    return lax.dot_general(left, right, (((1,), (1,)), ((), ())), preferred_element_type=jnp.float32)

def back_product(weight, grads):
    return lax.dot_general(weight, grads, (((0,), (0,)), ((), ())), preferred_element_type=jnp.float32)

def cell_gates(conv_bf, prior_bf, gate_weight, cand_weight, recur_weight):
    channels = conv_bf.shape[0]
    stacked = jnp.concatenate([conv_bf, prior_bf], axis=0)
    preact = jnp.dot(gate_weight, stacked, preferred_element_type=jnp.float32)
    update = jax.nn.sigmoid(preact[:channels])
    reset = jax.nn.sigmoid(preact[channels:])
    recurrent = jnp.dot(recur_weight, prior_bf, preferred_element_type=jnp.float32)
    candidate = jnp.tanh(jnp.dot(cand_weight, conv_bf, preferred_element_type=jnp.float32) + reset * recurrent)
    return (stacked, update, reset, recurrent, candidate)

def reverse_cell(flow_grad, prior_state, update, reset, recurrent, candidate, gate_weight, cand_weight, recur_weight):
    channels = update.shape[0]
    d_update = flow_grad * (candidate - prior_state)
    d_act = flow_grad * update * (1.0 - candidate * candidate)
    d_recur = d_act * reset
    gate_delta = jnp.concatenate([d_update * update * (1.0 - update), d_act * recurrent * reset * (1.0 - reset)], axis=0).astype(jnp.bfloat16)
    cand_delta = d_act.astype(jnp.bfloat16)
    recur_delta = d_recur.astype(jnp.bfloat16)
    reverse_in = back_product(gate_weight, gate_delta)
    dconv = (reverse_in[:channels] + back_product(cand_weight, cand_delta)).astype(jnp.bfloat16)
    carry = (1.0 - update) * flow_grad + reverse_in[channels:] + back_product(recur_weight, recur_delta)
    return (carry, dconv, gate_delta, cand_delta, recur_delta)

def to_blocks(coarse):
    split = coarse.reshape(COARSE, N_RANGE, RANGE_DEV // 4, N_AZIMUTH, AZIM_DEV // 4).transpose(1, 3, 0, 2, 4)
    return split.reshape(N_RANGE, N_AZIMUTH, COARSE, BLOCKS_SLICE, BLOCK).transpose(0, 1, 3, 2, 4)

def from_blocks(blocks):
    grid = blocks.transpose(0, 1, 3, 2, 4).reshape(N_RANGE, N_AZIMUTH, COARSE, RANGE_DEV // 4, AZIM_DEV // 4)
    return grid.transpose(2, 0, 3, 1, 4).reshape(COARSE, RANGE_CELLS * AZIM_CELLS // 16)

def reference(features, state_init, kernel, gate_weight, cand_weight, recur_weight, down_weight, owner_map, dest_map, cart_cot):
    cell_count = RANGE_CELLS * AZIM_CELLS
    hidden = state_init.reshape(CHANNELS, cell_count).astype(jnp.float32)
    padded_list = []
    conv_list = []
    hidden_list = [hidden]
    block_list = []
    for instant in range(SLICES):
        padded = framed(features[instant])
        conv_bf = depthwise(padded, kernel, RANGE_CELLS, AZIM_CELLS).astype(jnp.bfloat16).reshape(CHANNELS, cell_count)
        stacked, update, reset, recurrent, candidate = cell_gates(conv_bf, hidden.astype(jnp.bfloat16), gate_weight, cand_weight, recur_weight)
        hidden = (1.0 - update) * hidden + update * candidate
        coarse = jnp.dot(down_weight, patches(hidden.astype(jnp.bfloat16), RANGE_CELLS, AZIM_CELLS), preferred_element_type=jnp.float32).astype(jnp.bfloat16)
        block_list.append(to_blocks(coarse))
        padded_list.append(padded)
        conv_list.append(conv_bf)
        hidden_list.append(hidden)
    blocks = jnp.concatenate(block_list, axis=2)
    keys = owner_map * BLOCKS + dest_map
    onehot = (keys[:, :, :, None] == jnp.arange(N_RANGE * BLOCKS, dtype=jnp.int32)[None, None, None, :]).astype(jnp.float32)
    flat = blocks.reshape(N_RANGE, N_AZIMUTH, BLOCKS, COARSE * BLOCK).astype(jnp.float32)
    cartesian = jnp.einsum('rabk,rabx->akx', onehot, flat)
    cartesian = cartesian.reshape(N_AZIMUTH, N_RANGE, BLOCKS, COARSE, BLOCK).transpose(1, 0, 2, 3, 4)
    cot_flat = cart_cot.transpose(1, 0, 2, 3, 4).reshape(N_AZIMUTH, N_RANGE * BLOCKS, COARSE * BLOCK).astype(jnp.float32)
    backed = jnp.einsum('rabk,akx->rabx', onehot, cot_flat).astype(jnp.bfloat16)
    backed = backed.reshape(N_RANGE, N_AZIMUTH, BLOCKS, COARSE, BLOCK)
    carry = jnp.zeros((CHANNELS, cell_count), jnp.float32)
    grad_kernel = jnp.zeros((CHANNELS, 3, 3), jnp.float32)
    grad_gate = jnp.zeros((2 * CHANNELS, 2 * CHANNELS), jnp.float32)
    grad_cand = jnp.zeros((CHANNELS, CHANNELS), jnp.float32)
    grad_recur = jnp.zeros((CHANNELS, CHANNELS), jnp.float32)
    grad_down = jnp.zeros((COARSE, 16 * CHANNELS), jnp.float32)
    grad_list = [None] * SLICES
    flipped = kernel[:, ::-1, ::-1]
    for instant in range(SLICES - 1, -1, -1):
        prior_state = hidden_list[instant]
        prior_bf = prior_state.astype(jnp.bfloat16)
        conv_bf = conv_list[instant]
        stacked, update, reset, recurrent, candidate = cell_gates(conv_bf, prior_bf, gate_weight, cand_weight, recur_weight)
        next_bf = hidden_list[instant + 1].astype(jnp.bfloat16)
        d_coarse = from_blocks(backed[:, :, instant * BLOCKS_SLICE:(instant + 1) * BLOCKS_SLICE])
        grad_down = grad_down + cross_cells(d_coarse, patches(next_bf, RANGE_CELLS, AZIM_CELLS))
        flow_grad = carry + unpatches(back_product(down_weight, d_coarse), RANGE_CELLS, AZIM_CELLS)
        carry, dconv, gate_delta, cand_delta, recur_delta = reverse_cell(flow_grad, prior_state, update, reset, recurrent, candidate, gate_weight, cand_weight, recur_weight)
        grad_gate = grad_gate + cross_cells(gate_delta, stacked)
        grad_cand = grad_cand + cross_cells(cand_delta, conv_bf)
        grad_recur = grad_recur + cross_cells(recur_delta, prior_bf)
        dconv_grid = dconv.reshape(CHANNELS, RANGE_CELLS, AZIM_CELLS)
        grad_kernel = grad_kernel + kernel_terms(padded_list[instant], dconv_grid, RANGE_CELLS, AZIM_CELLS)
        grad_list[instant] = depthwise(framed(dconv_grid), flipped, RANGE_CELLS, AZIM_CELLS).astype(jnp.bfloat16)
    grad_scale = 1.0 / math.sqrt(SLICES * RANGE_CELLS * AZIM_CELLS)
    grad_features = jnp.stack(grad_list, axis=0)
    grad_state = carry.reshape(CHANNELS, RANGE_CELLS, AZIM_CELLS)
    return (cartesian, grad_features, grad_state, grad_kernel * grad_scale, grad_gate * grad_scale, grad_cand * grad_scale, grad_recur * grad_scale, grad_down * grad_scale)
```

```python
import functools
import math

import jax
import jax.numpy as jnp
from jax import lax
from jax.experimental import pallas as pl
from jax.experimental.pallas import tpu as pltpu
from jax.sharding import PartitionSpec as P

MESH = pl.DeviceIdType.MESH
F32 = jnp.float32
BF16 = jnp.bfloat16
I32 = jnp.int32

CH = 64
NT = 4
NROW = 16
NCOL = 128
CELLS = NROW * NCOL
NAT = CH * NROW
CO = 128
SPAN = 512
GROUP = 16


def iota(shape, dim):
    return lax.broadcasted_iota(I32, shape, dim)


def nn(left, right):
    return lax.dot_general(left, right, (((1,), (0,)), ((), ())), preferred_element_type=F32)


def nt(left, right):
    return lax.dot_general(left, right, (((1,), (1,)), ((), ())), preferred_element_type=F32)


def remote(src, dst, send_sem, recv_sem, device):
    return pltpu.make_async_remote_copy(
        src_ref=src,
        dst_ref=dst,
        send_sem=send_sem,
        recv_sem=recv_sem,
        device_id=device,
        device_id_type=MESH,
    )


def kernel(
    nr,
    na,
    scale,
    feat,
    state,
    kern,
    gate,
    cand,
    recur,
    down,
    owner,
    dest,
    cot,
    cart,
    gfeat,
    gstate,
    gkern,
    ggate,
    gcand,
    grecur,
    gdown,
    fx,
    xs,
    stk,
    hs,
    s_a,
    s_b,
    s_c,
    s_r,
    s_u,
    flow_in,
    pt,
    hcat,
    perm,
    pick,
    spread,
    wall,
    wall_t,
    wp,
    wb,
    wk,
    dlt,
    dcv,
    carry,
    dwacc,
    gkacc,
    gd,
    coracc,
    row_s,
    row_r,
    col_s,
    col_r,
    cor_s,
    cor_r,
    cot_all,
    key_all,
    blk_all,
    gds,
    gdr,
    gd2,
    gd2r,
    gd3,
    sm1s,
    sm1r,
    sm2,
    sm2r,
    sm3,
    halo_ss,
    halo_rs,
    cot_ss,
    cot_rs,
    key_ss,
    key_rs,
    blk_ss,
    blk_rs,
    xy_ss,
    xy_rs,
    z_ss,
    z_rs,
):
    r = lax.axis_index("range")
    a = lax.axis_index("azimuth")
    n2 = na // 2
    n1 = nr * 2
    k2 = a // 2
    zl = a % 2
    k1 = r * 2 + zl

    def ring_r(d):
        return lax.rem(r + d + nr, nr)

    def ring_a(d):
        return lax.rem(a + d + na, na)

    def xy_device(d):
        return (r, lax.rem(k2 + d, n2) * 2 + zl)

    def z_device(d):
        m = lax.rem(k1 + d, n1)
        return (m // 2, k2 * 2 + m % 2)

    barrier = pltpu.get_barrier_semaphore()

    def greet(device):
        pl.semaphore_signal(barrier, inc=1, device_id=device, device_id_type=MESH)

    diagonals = [(-1, -1), (-1, 1), (1, -1), (1, 1)]
    for da in (-1, 1):
        greet((r, ring_a(da)))
    for dr, da in diagonals:
        greet((ring_r(dr), ring_a(da)))

    def greet_xy(d, c):
        greet(xy_device(d))
        return c

    def greet_z(d, c):
        greet(z_device(d))
        return c

    lax.fori_loop(1, n2, greet_xy, 0)
    lax.fori_loop(1, n1, greet_z, 0)

    lane = iota((GROUP, NCOL), 1)
    lane8 = lane // 8
    lane16 = lane // 16

    def chans(g):
        return pl.ds(pl.multiple_of(g * GROUP, GROUP), GROUP)

    def feature_row(t, g, i):
        return fx[pl.ds(t * NAT + g * GROUP * NROW + i, GROUP, stride=NROW), :]

    def dconv_row(t, g, i):
        return dcv[t, chans(g), pl.ds(i * NCOL, NCOL)]

    def pack(ph, row):
        def step(n, c):
            t, g = n // 4, n % 4
            cs = chans(g)
            left = jnp.zeros((GROUP, NCOL), F32)
            right = jnp.zeros((GROUP, NCOL), F32)
            for i in range(NROW):
                x = row(t, g, i)
                y = pltpu.roll(x, (8 * i + 8) % NCOL, 1)
                right = jnp.where(lane8 == i, y, right)
                left = jnp.where(lane8 == (i + 1) % 16, y, left)
                if i in (0, NROW - 1):
                    end = 0 if i == 0 else 1
                    row_s[ph, end, t, cs, :] = x.astype(BF16)
                    spot = 2 * t + end
                    y = pltpu.roll(x, (16 * spot + 8) % NCOL, 1)
                    coracc[cs, :] = jnp.where(lane16 == spot, y, coracc[cs, :])
            col_s[ph, 0, t, cs, :] = pltpu.roll(left, NCOL - 16, 1).astype(BF16)
            col_s[ph, 1, t, cs, :] = right.astype(BF16)
            return c

        lax.fori_loop(0, 4 * NT, step, 0)
        cor_s[ph] = coracc[...].astype(BF16)

    def halo_copies(ph):
        copies = []
        for end, d in ((0, -1), (1, 1)):
            n = len(copies)
            copies.append(
                remote(
                    row_s.at[ph, end],
                    row_r.at[ph, 1 - end],
                    halo_ss.at[ph, n],
                    halo_rs.at[ph, n],
                    (ring_r(d), a),
                )
            )
        for end, d in ((0, -1), (1, 1)):
            n = len(copies)
            copies.append(
                remote(
                    col_s.at[ph, end],
                    col_r.at[ph, 1 - end],
                    halo_ss.at[ph, n],
                    halo_rs.at[ph, n],
                    (r, ring_a(d)),
                )
            )
        for j, (dr, da) in enumerate(diagonals):
            n = len(copies)
            copies.append(
                remote(
                    cor_s.at[ph],
                    cor_r.at[ph, 3 - j],
                    halo_ss.at[ph, n],
                    halo_rs.at[ph, n],
                    (ring_r(dr), ring_a(da)),
                )
            )
        return copies

    has_low = (r > 0).astype(F32)
    has_high = (r < nr - 1).astype(F32)

    def windows(ph, row, t, g):
        cs = chans(g)
        halo_l = col_r[ph, 0, t, cs, :].astype(F32)
        halo_h = col_r[ph, 1, t, cs, :].astype(F32)
        out = [[None] * (NROW + 2) for _ in range(3)]

        def put(pos, x, low, high):
            out[0][pos] = jnp.where(lane < 8, low, pltpu.roll(x, 8, 1))
            out[1][pos] = x
            out[2][pos] = jnp.where(lane >= NCOL - 8, high, pltpu.roll(x, NCOL - 8, 1))

        for i in range(NROW):
            x = row(t, g, i)
            w = pltpu.roll(jnp.where(lane8 == i, halo_l, halo_h), (NCOL - 8 * i) % NCOL, 1)
            put(i + 1, x, w, w)
        for end in (0, 1):
            keep = has_low if end == 0 else has_high
            spot = 2 * t + (1 - end)
            x = row_r[ph, end, t, cs, :].astype(F32) * keep
            c_l = cor_r[ph, 2 * end, cs, :].astype(F32) * keep
            c_h = cor_r[ph, 2 * end + 1, cs, :].astype(F32) * keep
            low = pltpu.roll(c_l, lax.rem(NCOL - 16 * spot, NCOL), 1)
            high = pltpu.roll(c_h, 112 - 16 * spot, 1)
            put(0 if end == 0 else NROW + 1, x, low, high)
        return out

    def convolve(shifted, g, flipped, store):
        cs = chans(g)
        taps = [wk[8 - n if flipped else n, cs, :] for n in range(9)]
        for i in range(NROW):
            total = taps[0] * shifted[0][i]
            for n in range(1, 9):
                total = total + taps[n] * shifted[n % 3][i + n // 3]
            store(i, total)

    def widen(n, c):
        at = pl.ds(pl.multiple_of(n * 256, 256), 256)
        fx[at, :] = feat[at, :].astype(F32)
        return c

    lax.fori_loop(0, NT * NAT // 256, widen, 0)
    coracc[...] = jnp.zeros((CH, NCOL), F32)
    pack(0, feature_row)
    key_row = iota((8, NCOL), 0)
    keys = jnp.zeros((8, NCOL), I32)
    for b in range(NT):
        keys = jnp.where(key_row == b, owner[0, 0, b] * NT + dest[0, 0, b], keys)
    key_all[r] = keys

    pl.semaphore_wait(barrier, 6 + (n2 - 1) + (n1 - 1))

    halo0 = halo_copies(0)
    for copy in halo0:
        copy.start()
    cot_copies = []
    key_copies = []
    for d in range(1, nr):
        device = (ring_r(d), a)
        key_copies.append(
            remote(key_all.at[r], key_all.at[r], key_ss.at[d - 1], key_rs.at[d - 1], device)
        )
        cot_copies.append(remote(cot, cot_all.at[r], cot_ss.at[d - 1], cot_rs.at[d - 1], device))
    for copy in cot_copies + key_copies:
        copy.start()

    cot_all[r] = cot[...]

    def make_perm(n, c):
        at = pl.multiple_of(n * 128, 128)
        src = iota((128, 1), 0) + at
        to = (src % 4) * 256 + ((src // 4) % 4) * CH + src // 16
        perm[pl.ds(at, 128), :] = (iota((128, 1024), 1) == to).astype(F32).astype(BF16)
        return c

    lax.fori_loop(0, 8, make_perm, 0)

    def make_pick(n, c):
        at = pl.multiple_of(n * 128, 128)
        src = iota((128, 1), 0) + at
        to = (src % 4) * 128 + (src // 128) * 32 + (src % 128) // 4
        pick[pl.ds(at, 128), :] = (iota((128, SPAN), 1) == to).astype(F32).astype(BF16)
        return c

    lax.fori_loop(0, 4, make_pick, 0)
    dst = iota((128, SPAN), 1)
    spread[...] = (iota((128, SPAN), 0) == (dst // 128) * 32 + (dst % 128) // 4).astype(F32).astype(BF16)

    place = iota((CH, 2 * CH), 1) - iota((CH, 2 * CH), 0)
    wall[0 : 2 * CH, :] = gate[...]
    wall[2 * CH : 3 * CH, :] = nn(cand[...], (place == 0).astype(F32).astype(BF16)).astype(BF16)
    wall[3 * CH : 4 * CH, :] = nn(recur[...], (place == CH).astype(F32).astype(BF16)).astype(BF16)
    wall_t[...] = wall[...].astype(F32).T.astype(BF16)
    for q in range(4):
        part = nn(down[...], perm[:, q * 256 : (q + 1) * 256])
        wp[:, q * 256 : (q + 1) * 256] = part.astype(BF16)
        wb[:, q * 128 : (q + 1) * 128] = part.T.astype(BF16)
    for n in range(9):
        line = kern[n // 3, n % 3 : n % 3 + 1, :]
        wk[n] = jnp.broadcast_to(line, (NCOL, CH)).T
    gstate[...] = state[...].astype(F32)
    for i in range(NROW):
        hs[0, :, i * NCOL : (i + 1) * NCOL] = gstate[pl.ds(i, CH, stride=NROW), :]

    for copy in halo0:
        copy.wait_recv()

    def conv_forward(n, c):
        t, g = n // 4, n % 4
        cs = chans(g)
        shifted = windows(0, feature_row, t, g)
        for b in range(3):
            for i in range(NROW + 2):
                xs[t, b, i, cs, :] = shifted[b][i]

        def store(i, total):
            stk[t, cs, i * NCOL : (i + 1) * NCOL] = total.astype(BF16)

        convolve(shifted, g, False, store)
        return c

    lax.fori_loop(0, 4 * NT, conv_forward, 0)

    def forward(t, c):
        for ic in range(4):
            ls = slice(ic * SPAN, (ic + 1) * SPAN)
            h = hs[t, :, ls]
            stk[t, CH : 2 * CH, ls] = h.astype(BF16)
            pre = nn(wall[...], stk[t, :, ls])
            u = 0.5 * jnp.tanh(0.5 * pre[0:CH]) + 0.5
            z = 0.5 * jnp.tanh(0.5 * pre[CH : 2 * CH]) + 0.5
            rec = pre[3 * CH : 4 * CH]
            act = jnp.tanh(pre[2 * CH : 3 * CH] + z * rec)
            gap = act - h
            step = u * gap
            new = h + step
            hs[t + 1, :, ls] = new
            s_u[t, :, ls] = u
            s_r[t, :, ls] = z
            s_a[t, :, ls] = step * (1.0 - u)
            s_b[t, :, ls] = u * (1.0 - act * act)
            s_c[t, :, ls] = rec * z * (1.0 - z)
            new_bf = new.astype(BF16)
            for p in range(4):
                hcat[p * CH : (p + 1) * CH, ic * NCOL : (ic + 1) * NCOL] = new_bf[
                    :, p * NCOL : (p + 1) * NCOL
                ]
        sorted_lanes = nn(hcat[...], pick[...])
        for q in range(4):
            pt[t, q * 256 : (q + 1) * 256, :] = sorted_lanes[:, q * 128 : (q + 1) * 128].astype(BF16)
        blk_all[r, t] = nn(wp[...], pt[t]).astype(BF16)
        return c

    for t in range(NT):
        forward(t, 0)

    blk_copies = []
    for d in range(1, nr):
        device = (ring_r(d), a)
        blk_copies.append(
            remote(blk_all.at[r], blk_all.at[r], blk_ss.at[d - 1], blk_rs.at[d - 1], device)
        )
    for copy in blk_copies:
        copy.start()

    for copy in cot_copies:
        copy.wait_recv()
    gd[...] = jnp.zeros(gd.shape, F32)
    sub = iota((CO, SPAN), 1) % 4

    def coarse_back(t, c):
        block = cot_all[owner[0, 0, t], dest[0, 0, t]]
        wide = nn(block, spread[...])
        each = [jnp.where(sub == q, wide, 0.0).astype(BF16) for q in range(4)]
        flow_in[t] = nn(wb[...], jnp.concatenate(each, axis=0))
        gd[...] += nt(block, pt[t])
        return c

    for t in range(NT):
        coarse_back(t, 0)

    fold_rows, fold_cols = gds.shape[1], gds.shape[2]
    own_rows = CO // n2
    parts = fold_rows // own_rows
    natural = nt(gd[...].astype(BF16), perm[...])
    for k in range(n2):
        mine = natural[k * own_rows : (k + 1) * own_rows]
        gds[k] = jnp.concatenate(
            [mine[:, j * fold_cols : (j + 1) * fold_cols] for j in range(parts)], axis=0
        ).astype(BF16)

    def start_all(count, make):
        def go(d, c):
            make(d).start()
            return c

        lax.fori_loop(1, count, go, 0)

    def wait_all(count, make):
        def go(d, c):
            make(d).wait_recv()
            return c

        lax.fori_loop(1, count, go, 0)

    def sent_all(count, make):
        def go(d, c):
            make(d).wait_send()
            return c

        lax.fori_loop(1, count, go, 0)

    def scatter_copy(slot, src, dst):
        def make(d):
            to = lax.rem(k2 + d, n2)
            return remote(
                src(to), dst.at[d - 1], xy_ss.at[slot, d - 1], xy_rs.at[slot, d - 1], xy_device(d)
            )

        return make

    def z_copy(slot, src, dst):
        def make(d):
            return remote(src, dst.at[d - 1], z_ss.at[slot, d - 1], z_rs.at[slot, d - 1], z_device(d))

        return make

    def gather_copy(slot, buf):
        def make(d):
            return remote(
                buf.at[k2], buf.at[k2], xy_ss.at[slot, d - 1], xy_rs.at[slot, d - 1], xy_device(d)
            )

        return make

    big1 = scatter_copy(0, lambda to: gds.at[to], gdr)
    big2 = z_copy(0, gd2, gd2r)
    big3 = gather_copy(1, gd3)
    sm_rows = 4 * CH // n2
    small1 = scatter_copy(
        2, lambda to: sm1s.at[pl.ds(pl.multiple_of(to * sm_rows, sm_rows), sm_rows)], sm1r
    )
    small2 = z_copy(1, sm2, sm2r)
    small3 = gather_copy(3, sm3)

    def sum_slots(own, buf, count):
        def add(d, total):
            return total + buf[d].astype(F32)

        return lax.fori_loop(0, count, add, own)

    start_all(n2, big1)

    def big_second():
        wait_all(n2, big1)
        gd2[...] = sum_slots(gds[k2].astype(F32), gdr, n2 - 1)
        start_all(n1, big2)

    def big_third():
        wait_all(n1, big2)
        total = sum_slots(gd2[...], gd2r, n1 - 1) * scale
        gd3[k2] = jnp.concatenate(
            [total[j * own_rows : (j + 1) * own_rows] for j in range(parts)], axis=1
        )
        start_all(n2, big3)

    carry[...] = jnp.zeros(carry.shape, F32)
    dwacc[...] = jnp.zeros(dwacc.shape, F32)
    gkacc[...] = jnp.zeros(gkacc.shape, F32)

    def backward(n, c):
        t = NT - 1 - n
        for ic in range(4):
            ls = slice(ic * SPAN, (ic + 1) * SPAN)
            rows_in = [
                flow_in[t, p * CH : (p + 1) * CH, ic * NCOL : (ic + 1) * NCOL] for p in range(4)
            ]
            flow = carry[:, ls] + jnp.concatenate(rows_in, axis=1)
            act = flow * s_b[t, :, ls]
            dlt[0:CH, ls] = (flow * s_a[t, :, ls]).astype(BF16)
            dlt[CH : 2 * CH, ls] = (act * s_c[t, :, ls]).astype(BF16)
            dlt[2 * CH : 3 * CH, ls] = act.astype(BF16)
            dlt[3 * CH : 4 * CH, ls] = (act * s_r[t, :, ls]).astype(BF16)
            rev = nn(wall_t[...], dlt[:, ls])
            dcv[t, :, ls] = rev[0:CH].astype(BF16).astype(F32)
            carry[:, ls] = (1.0 - s_u[t, :, ls]) * flow + rev[CH : 2 * CH]
        dwacc[...] += nt(dlt[...], stk[t])

        def kernel_grad(g, c2):
            cs = chans(g)
            grads = [dcv[t, cs, i * NCOL : (i + 1) * NCOL] for i in range(NROW)]
            for tap in range(9):
                total = gkacc[tap, cs, :]
                for i in range(NROW):
                    total = total + grads[i] * xs[t, tap % 3, i + tap // 3, cs, :]
                gkacc[tap, cs, :] = total
            return c2

        lax.fori_loop(0, 4, kernel_grad, 0)
        pl.when(n == 1)(big_second)
        pl.when(n == 3)(big_third)
        return c

    lax.fori_loop(0, NT, backward, 0)

    lanes = iota((CH, NCOL), 1)
    sm1s[0 : 2 * CH, :] = dwacc[0 : 2 * CH, :]
    sm1s[2 * CH : 3 * CH, :] = jnp.where(
        lanes < CH, dwacc[2 * CH : 3 * CH, :], dwacc[3 * CH : 4 * CH, :]
    )
    columns = jnp.zeros((CH, NCOL), F32)
    for tap in range(9):
        columns = jnp.where(lanes == tap, jnp.sum(gkacc[tap], axis=1, keepdims=True), columns)
    sm1s[3 * CH : 4 * CH, :] = columns
    start_all(n2, small1)

    coracc[...] = jnp.zeros((CH, NCOL), F32)
    pack(1, dconv_row)
    halo1 = halo_copies(1)
    for copy in halo1:
        copy.start()

    for i in range(NROW):
        gstate[pl.ds(i, CH, stride=NROW), :] = carry[:, i * NCOL : (i + 1) * NCOL]

    wait_all(n2, small1)
    own = sm1s[pl.ds(pl.multiple_of(k2 * sm_rows, sm_rows), sm_rows), :]
    sm2[...] = sum_slots(own, sm1r, n2 - 1)
    start_all(n1, small2)

    for copy in key_copies + blk_copies:
        copy.wait_recv()

    def gather_blocks(n, c):
        at = pl.ds(pl.multiple_of(n * 32, 32), 32)
        totals = [jnp.zeros((32, NCOL), F32) for _ in range(NT)]
        for src in range(nr):
            for b in range(NT):
                key = key_all[src, b : b + 1, :]
                block = blk_all[src, b, at, :].astype(F32)
                for d in range(NT):
                    totals[d] = totals[d] + jnp.where(key == r * NT + d, block, 0.0)
        for d in range(NT):
            cart[d, at, :] = totals[d]
        return c

    lax.fori_loop(0, 4, gather_blocks, 0)

    wait_all(n1, small2)
    sm3[k2] = sum_slots(sm2[...], sm2r, n1 - 1) * scale
    start_all(n2, small3)

    for copy in halo1:
        copy.wait_recv()

    def conv_backward(n, c):
        t, g = n // 4, n % 4
        shifted = windows(1, dconv_row, t, g)

        def store(i, total):
            fx[pl.ds(t * NAT + g * GROUP * NROW + i, GROUP, stride=NROW), :] = total

        convolve(shifted, g, True, store)
        at = pl.ds(pl.multiple_of(n * 256, 256), 256)
        gfeat[at, :] = fx[at, :].astype(BF16)
        return c

    lax.fori_loop(0, 4 * NT, conv_backward, 0)

    wait_all(n2, big3)
    gdown[...] = gd3[...].reshape(CO, 16 * CH)

    wait_all(n2, small3)
    small = sm3[...].reshape(4 * CH, NCOL)
    ggate[...] = small[0 : 2 * CH]
    middle = small[2 * CH : 3 * CH]
    gcand[...] = middle[:, 0:CH]
    grecur[...] = pltpu.roll(middle, CH, 1)[:, 0:CH]
    lines = small[3 * CH : 4 * CH].T
    for tap in range(9):
        gkern[tap // 3, tap % 3 : tap % 3 + 1, :] = lines[tap : tap + 1, :]

    for copy in halo0 + halo1 + cot_copies + key_copies + blk_copies:
        copy.wait_send()
    sent_all(n2, big1)
    sent_all(n1, big2)
    sent_all(n2, big3)
    sent_all(n2, small1)
    sent_all(n1, small2)
    sent_all(n2, small3)


def on_device(nr, na, *args):
    (features, state_init, kern, gate, cand, recur, down, owner_map, dest_map, cart_cot) = args
    scale = 1.0 / math.sqrt(NT * CELLS * nr * na)
    n2, n1 = na // 2, nr * 2
    own_rows = CO // n2
    parts = max(1, 16 // own_rows)
    fold = (own_rows * parts, 16 * CH // parts)
    sm_rows = 4 * CH // n2
    vmem = pl.BlockSpec(memory_space=pltpu.VMEM)
    smem = pl.BlockSpec(memory_space=pltpu.SMEM)
    dma = pltpu.SemaphoreType.DMA
    cells = (NT, CH, CELLS)
    scratch = [
        pltpu.VMEM((NT * NAT, NCOL), F32),
        pltpu.VMEM((NT, 3, NROW + 2, CH, NCOL), F32),
        pltpu.VMEM((NT, 2 * CH, CELLS), BF16),
        pltpu.VMEM((NT + 1, CH, CELLS), F32),
        pltpu.VMEM(cells, F32),
        pltpu.VMEM(cells, F32),
        pltpu.VMEM(cells, F32),
        pltpu.VMEM(cells, F32),
        pltpu.VMEM(cells, F32),
        pltpu.VMEM((NT, 4 * CH, SPAN), F32),
        pltpu.VMEM((NT, 16 * CH, 128), BF16),
        pltpu.VMEM((4 * CH, SPAN), BF16),
        pltpu.VMEM((1024, 1024), BF16),
        pltpu.VMEM((SPAN, SPAN), BF16),
        pltpu.VMEM((128, SPAN), BF16),
        pltpu.VMEM((4 * CH, 2 * CH), BF16),
        pltpu.VMEM((2 * CH, 4 * CH), BF16),
        pltpu.VMEM((CO, 16 * CH), BF16),
        pltpu.VMEM((4 * CH, 4 * CO), BF16),
        pltpu.VMEM((9, CH, NCOL), F32),
        pltpu.VMEM((4 * CH, CELLS), BF16),
        pltpu.VMEM(cells, F32),
        pltpu.VMEM((CH, CELLS), F32),
        pltpu.VMEM((4 * CH, 2 * CH), F32),
        pltpu.VMEM((9, CH, NCOL), F32),
        pltpu.VMEM((CO, 16 * CH), F32),
        pltpu.VMEM((CH, NCOL), F32),
        pltpu.VMEM((2, 2, NT, CH, NCOL), BF16),
        pltpu.VMEM((2, 2, NT, CH, NCOL), BF16),
        pltpu.VMEM((2, 2, NT, CH, NCOL), BF16),
        pltpu.VMEM((2, 2, NT, CH, NCOL), BF16),
        pltpu.VMEM((2, CH, NCOL), BF16),
        pltpu.VMEM((2, 4, CH, NCOL), BF16),
        pltpu.VMEM((nr, NT, CO, 128), BF16),
        pltpu.VMEM((nr, 8, 128), I32),
        pltpu.VMEM((nr, NT, CO, 128), BF16),
        pltpu.VMEM((n2, *fold), BF16),
        pltpu.VMEM((n2 - 1, *fold), BF16),
        pltpu.VMEM(fold, F32),
        pltpu.VMEM((n1 - 1, *fold), F32),
        pltpu.VMEM((n2, own_rows, 16 * CH), F32),
        pltpu.VMEM((4 * CH, NCOL), F32),
        pltpu.VMEM((n2 - 1, sm_rows, NCOL), F32),
        pltpu.VMEM((sm_rows, NCOL), F32),
        pltpu.VMEM((n1 - 1, sm_rows, NCOL), F32),
        pltpu.VMEM((n2, sm_rows, NCOL), F32),
        dma((2, 8)),
        dma((2, 8)),
        dma((nr - 1,)),
        dma((nr - 1,)),
        dma((nr - 1,)),
        dma((nr - 1,)),
        dma((nr - 1,)),
        dma((nr - 1,)),
        dma((4, n2 - 1)),
        dma((4, n2 - 1)),
        dma((2, n1 - 1)),
        dma((2, n1 - 1)),
    ]
    out = pl.pallas_call(
        functools.partial(kernel, nr, na, scale),
        out_shape=(
            jax.ShapeDtypeStruct((NT, CO, 128), F32),
            jax.ShapeDtypeStruct((NT * NAT, NCOL), BF16),
            jax.ShapeDtypeStruct((NAT, NCOL), F32),
            jax.ShapeDtypeStruct((3, 3, CH), F32),
            jax.ShapeDtypeStruct((2 * CH, 2 * CH), F32),
            jax.ShapeDtypeStruct((CH, CH), F32),
            jax.ShapeDtypeStruct((CH, CH), F32),
            jax.ShapeDtypeStruct((CO, 16 * CH), F32),
        ),
        in_specs=[vmem] * 7 + [smem] * 2 + [vmem],
        out_specs=(vmem,) * 8,
        scratch_shapes=scratch,
        compiler_params=pltpu.CompilerParams(
            collective_id=0, has_side_effects=True, vmem_limit_bytes=60 * 1024 * 1024
        ),
        name="section",
    )(
        features.reshape(NT * NAT, NCOL),
        state_init.reshape(NAT, NCOL),
        kern.transpose(1, 2, 0),
        gate,
        cand,
        recur,
        down,
        owner_map,
        dest_map,
        cart_cot.reshape(NT, CO, 128),
    )
    cart, gfeat, gstate, gkern, ggate, gcand, grecur, gdown = out
    return (
        cart.reshape(1, 1, NT, CO, 128),
        gfeat.reshape(NT, CH, NROW, NCOL),
        gstate.reshape(CH, NROW, NCOL),
        gkern.transpose(2, 0, 1),
        ggate,
        gcand,
        grecur,
        gdown,
    )


def solution(mesh):
    nr, na = mesh.shape["range"], mesh.shape["azimuth"]
    tile = P(None, "range", "azimuth")
    maps = P("range", "azimuth", None)
    cartesian = P("range", "azimuth", None, None, None)
    features = P(None, None, "range", "azimuth")
    return jax.shard_map(
        functools.partial(on_device, nr, na),
        mesh=mesh,
        in_specs=(features, tile, P(), P(), P(), P(), P(), maps, maps, cartesian),
        out_specs=(cartesian, features, tile, P(), P(), P(), P(), P()),
        check_vma=False,
    )
```

```python
import functools
import math

import jax
import jax.numpy as jnp
from jax import lax
from jax.experimental import pallas as pl
from jax.experimental.pallas import tpu as pltpu
from jax.sharding import PartitionSpec as P

MESH = pl.DeviceIdType.MESH
F32 = jnp.float32
BF16 = jnp.bfloat16
I32 = jnp.int32

CH = 64
NT = 4
NROW = 16
NCOL = 128
CELLS = NROW * NCOL
NAT = CH * NROW
CO = 128
SPAN = 512
GROUP = 16


def iota(shape, dim):
    return lax.broadcasted_iota(I32, shape, dim)


def nn(left, right):
    return lax.dot_general(left, right, (((1,), (0,)), ((), ())), preferred_element_type=F32)


def nt(left, right):
    return lax.dot_general(left, right, (((1,), (1,)), ((), ())), preferred_element_type=F32)


def remote(src, dst, send_sem, recv_sem, device):
    return pltpu.make_async_remote_copy(
        src_ref=src,
        dst_ref=dst,
        send_sem=send_sem,
        recv_sem=recv_sem,
        device_id=device,
        device_id_type=MESH,
    )


def kernel(
    nr,
    na,
    scale,
    feat_in,
    state_in,
    kern_in,
    gate_in,
    cand_in,
    recur_in,
    down_in,
    owner,
    dest,
    cot_in,
    cart,
    gfeat,
    gstate,
    gkern,
    ggate,
    gcand,
    grecur,
    gdown,
    feat,
    state,
    kern,
    cand,
    recur,
    down,
    fx,
    xs,
    stk,
    hs,
    s_a,
    s_b,
    s_c,
    s_r,
    s_u,
    flow_in,
    pt,
    hcat,
    perm,
    pick,
    spread,
    wall,
    wall_t,
    wp,
    wb,
    wk,
    dlt,
    dcv,
    carry,
    dwacc,
    gkacc,
    gd,
    row_s,
    row_r,
    col_s,
    col_r,
    cor_s,
    cor_r,
    cot_all,
    key_all,
    blk_all,
    gds,
    gdr,
    gd2,
    gd2r,
    gd3,
    sm1s,
    sm1r,
    sm2,
    sm2r,
    sm3,
    in_sem,
    halo_ss,
    halo_rs,
    cot_ss,
    cot_rs,
    key_ss,
    key_rs,
    blk_ss,
    blk_rs,
    xy_ss,
    xy_rs,
    z_ss,
    z_rs,
):
    r = lax.axis_index("range")
    a = lax.axis_index("azimuth")
    n2 = na // 2
    n1 = nr * 2
    k2 = a // 2
    zl = a % 2
    k1 = r * 2 + zl

    def ring_r(d):
        return lax.rem(r + d + nr, nr)

    def ring_a(d):
        return lax.rem(a + d + na, na)

    def xy_device(d):
        return (r, lax.rem(k2 + d, n2) * 2 + zl)

    def z_device(d):
        m = lax.rem(k1 + d, n1)
        return (m // 2, k2 * 2 + m % 2)

    barrier = pltpu.get_barrier_semaphore()

    def greet(device):
        pl.semaphore_signal(barrier, inc=1, device_id=device, device_id_type=MESH)

    diagonals = [(-1, -1), (-1, 1), (1, -1), (1, 1)]
    for da in (-1, 1):
        greet((r, ring_a(da)))
    for dr, da in diagonals:
        greet((ring_r(dr), ring_a(da)))

    def greet_xy(d, c):
        greet(xy_device(d))
        return c

    def greet_z(d, c):
        greet(z_device(d))
        return c

    lax.fori_loop(1, n2, greet_xy, 0)
    lax.fori_loop(1, n1, greet_z, 0)

    fetches = [
        pltpu.make_async_copy(src, dst, in_sem.at[n])
        for n, (src, dst) in enumerate(
            (
                (feat_in, feat),
                (state_in, state),
                (kern_in, kern),
                (gate_in, wall.at[pl.ds(0, 2 * CH)]),
                (cand_in, cand),
                (recur_in, recur),
                (down_in, down),
                (cot_in, cot_all.at[r]),
            )
        )
    ]
    for fetch in fetches:
        fetch.start()

    lane = iota((GROUP, NCOL), 1)
    lane8 = lane // 8
    lane16 = lane // 16

    def chans(g):
        return pl.ds(pl.multiple_of(g * GROUP, GROUP), GROUP)

    def feature_row(t, g, i):
        return fx[pl.ds(t * NAT + g * GROUP * NROW + i, GROUP, stride=NROW), :]

    def dconv_row(t, g, i):
        return dcv[t, chans(g), pl.ds(i * NCOL, NCOL)]

    def pack(ph, row):
        def step(g, c):
            cs = chans(g)
            corner = jnp.zeros((GROUP, NCOL), F32)
            for t in range(NT):
                left = jnp.zeros((GROUP, NCOL), F32)
                right = jnp.zeros((GROUP, NCOL), F32)
                for i in range(NROW):
                    x = row(t, g, i)
                    y = pltpu.roll(x, 8 * i + 8, 1) if i < NROW - 1 else x
                    right = jnp.where(lane8 == i, y, right)
                    left = jnp.where(lane8 == (i + 1) % 16, y, left)
                    if i == 0:
                        row_s[ph, 0, t, cs, :] = x.astype(BF16)
                        y = pltpu.roll(x, 32 * t + 8, 1)
                        corner = jnp.where(lane16 == 2 * t, y, corner)
                    if i == NROW - 1:
                        row_s[ph, 1, t, cs, :] = x.astype(BF16)
                        y = pltpu.roll(x, (32 * t + 24) % NCOL, 1)
                        corner = jnp.where(lane16 == 2 * t + 1, y, corner)
                col_s[ph, 0, t, cs, :] = pltpu.roll(left, NCOL - 16, 1).astype(BF16)
                col_s[ph, 1, t, cs, :] = right.astype(BF16)
            cor_s[ph, cs, :] = corner.astype(BF16)
            return c

        lax.fori_loop(0, 4, step, 0)

    def halo_copies(ph):
        copies = []
        for end, d in ((0, -1), (1, 1)):
            n = len(copies)
            copies.append(
                remote(
                    row_s.at[ph, end],
                    row_r.at[ph, 1 - end],
                    halo_ss.at[ph, n],
                    halo_rs.at[ph, n],
                    (ring_r(d), a),
                )
            )
        for end, d in ((0, -1), (1, 1)):
            n = len(copies)
            copies.append(
                remote(
                    col_s.at[ph, end],
                    col_r.at[ph, 1 - end],
                    halo_ss.at[ph, n],
                    halo_rs.at[ph, n],
                    (r, ring_a(d)),
                )
            )
        for j, (dr, da) in enumerate(diagonals):
            n = len(copies)
            copies.append(
                remote(
                    cor_s.at[ph],
                    cor_r.at[ph, 3 - j],
                    halo_ss.at[ph, n],
                    halo_rs.at[ph, n],
                    (ring_r(dr), ring_a(da)),
                )
            )
        return copies

    has_low = (r > 0).astype(F32)
    has_high = (r < nr - 1).astype(F32)

    def windows(ph, row, t, g):
        cs = chans(g)
        halo_l = col_r[ph, 0, t, cs, :].astype(F32)
        halo_h = col_r[ph, 1, t, cs, :].astype(F32)
        out = [[None] * (NROW + 2) for _ in range(3)]

        def put(pos, x, low, high):
            out[0][pos] = jnp.where(lane < 8, low, pltpu.roll(x, 8, 1))
            out[1][pos] = x
            out[2][pos] = jnp.where(lane >= NCOL - 8, high, pltpu.roll(x, NCOL - 8, 1))

        for i in range(NROW):
            x = row(t, g, i)
            w = pltpu.roll(jnp.where(lane8 == i, halo_l, halo_h), (NCOL - 8 * i) % NCOL, 1)
            put(i + 1, x, w, w)
        for end in (0, 1):
            keep = has_low if end == 0 else has_high
            spot = 2 * t + (1 - end)
            x = row_r[ph, end, t, cs, :].astype(F32) * keep
            c_l = cor_r[ph, 2 * end, cs, :].astype(F32) * keep
            c_h = cor_r[ph, 2 * end + 1, cs, :].astype(F32) * keep
            low = pltpu.roll(c_l, lax.rem(NCOL - 16 * spot, NCOL), 1)
            high = pltpu.roll(c_h, 112 - 16 * spot, 1)
            put(0 if end == 0 else NROW + 1, x, low, high)
        return out

    def convolve(shifted, g, flipped, store):
        cs = chans(g)
        taps = [wk[8 - n if flipped else n, cs, :] for n in range(9)]
        for i in range(NROW):
            total = taps[0] * shifted[0][i]
            for n in range(1, 9):
                total = total + taps[n] * shifted[n % 3][i + n // 3]
            store(i, total)

    def widen(n, c):
        at = pl.ds(pl.multiple_of(n * 256, 256), 256)
        fx[at, :] = feat[at, :].astype(F32)
        return c

    fetches[0].wait()
    lax.fori_loop(0, NT * NAT // 256, widen, 0)
    pack(0, feature_row)
    key_row = iota((8, NCOL), 0)
    keys = jnp.zeros((8, NCOL), I32)
    for b in range(NT):
        keys = jnp.where(key_row == b, owner[0, 0, b] * NT + dest[0, 0, b], keys)
    key_all[r] = keys

    pl.semaphore_wait(barrier, 6 + (n2 - 1) + (n1 - 1))

    halo0 = halo_copies(0)
    for copy in halo0:
        copy.start()
    cot_copies = []
    key_copies = []
    for d in range(1, nr):
        device = (ring_r(d), a)
        key_copies.append(
            remote(key_all.at[r], key_all.at[r], key_ss.at[d - 1], key_rs.at[d - 1], device)
        )
        cot_copies.append(
            remote(cot_all.at[r], cot_all.at[r], cot_ss.at[d - 1], cot_rs.at[d - 1], device)
        )


    def make_perm(n, c):
        at = pl.multiple_of(n * 128, 128)
        src = iota((128, 1), 0) + at
        to = (src % 4) * 256 + ((src // 4) % 4) * CH + src // 16
        perm[pl.ds(at, 128), :] = (iota((128, 1024), 1) == to).astype(F32).astype(BF16)
        return c

    lax.fori_loop(0, 8, make_perm, 0)

    def make_pick(n, c):
        at = pl.multiple_of(n * 128, 128)
        src = iota((128, 1), 0) + at
        to = (src % 4) * 128 + (src // 128) * 32 + (src % 128) // 4
        pick[pl.ds(at, 128), :] = (iota((128, SPAN), 1) == to).astype(F32).astype(BF16)
        return c

    lax.fori_loop(0, 4, make_pick, 0)
    dst = iota((128, SPAN), 1)
    spread[...] = (iota((128, SPAN), 0) == (dst // 128) * 32 + (dst % 128) // 4).astype(F32).astype(BF16)

    place = iota((CH, 2 * CH), 1) - iota((CH, 2 * CH), 0)
    for fetch in fetches[1:]:
        fetch.wait()
    for copy in cot_copies + key_copies:
        copy.start()
    wall[2 * CH : 3 * CH, :] = nn(cand[...], (place == 0).astype(F32).astype(BF16)).astype(BF16)
    wall[3 * CH : 4 * CH, :] = nn(recur[...], (place == CH).astype(F32).astype(BF16)).astype(BF16)
    wall_t[...] = wall[...].astype(F32).T.astype(BF16)
    for q in range(4):
        part = nn(down[...], perm[:, q * 256 : (q + 1) * 256])
        wp[:, q * 256 : (q + 1) * 256] = part.astype(BF16)
        wb[:, q * 128 : (q + 1) * 128] = part.T.astype(BF16)
    for n in range(9):
        line = kern[n // 3, n % 3 : n % 3 + 1, :]
        wk[n] = jnp.broadcast_to(line, (NCOL, CH)).T
    gstate[...] = state[...].astype(F32)
    for i in range(NROW):
        hs[0, :, i * NCOL : (i + 1) * NCOL] = gstate[pl.ds(i, CH, stride=NROW), :]

    for copy in halo0:
        copy.wait_recv()

    def conv_forward(n, c):
        t, g = n // 4, n % 4
        cs = chans(g)
        shifted = windows(0, feature_row, t, g)
        for b in range(3):
            for i in range(NROW + 2):
                xs[t, b, i, cs, :] = shifted[b][i]

        def store(i, total):
            stk[t, cs, i * NCOL : (i + 1) * NCOL] = total.astype(BF16)

        convolve(shifted, g, False, store)
        return c

    lax.fori_loop(0, 4 * NT, conv_forward, 0)

    def forward(t, c):
        for ic in range(4):
            ls = slice(ic * SPAN, (ic + 1) * SPAN)
            h = hs[t, :, ls]
            stk[t, CH : 2 * CH, ls] = h.astype(BF16)
            pre = nn(wall[...], stk[t, :, ls])
            u = 0.5 * jnp.tanh(0.5 * pre[0:CH]) + 0.5
            z = 0.5 * jnp.tanh(0.5 * pre[CH : 2 * CH]) + 0.5
            rec = pre[3 * CH : 4 * CH]
            act = jnp.tanh(pre[2 * CH : 3 * CH] + z * rec)
            gap = act - h
            step = u * gap
            new = h + step
            hs[t + 1, :, ls] = new
            s_u[t, :, ls] = u
            s_r[t, :, ls] = z
            s_a[t, :, ls] = step * (1.0 - u)
            s_b[t, :, ls] = u * (1.0 - act * act)
            s_c[t, :, ls] = rec * z * (1.0 - z)
            new_bf = new.astype(BF16)
            for p in range(4):
                hcat[p * CH : (p + 1) * CH, ic * NCOL : (ic + 1) * NCOL] = new_bf[
                    :, p * NCOL : (p + 1) * NCOL
                ]
        sorted_lanes = nn(hcat[...], pick[...])
        for q in range(4):
            pt[t, q * 256 : (q + 1) * 256, :] = sorted_lanes[:, q * 128 : (q + 1) * 128].astype(BF16)
        blk_all[r, t] = nn(wp[...], pt[t]).astype(BF16)
        return c

    for t in range(NT):
        forward(t, 0)

    blk_copies = []
    for d in range(1, nr):
        device = (ring_r(d), a)
        blk_copies.append(
            remote(blk_all.at[r], blk_all.at[r], blk_ss.at[d - 1], blk_rs.at[d - 1], device)
        )
    for copy in blk_copies:
        copy.start()

    for copy in cot_copies:
        copy.wait_recv()
    gd[...] = jnp.zeros(gd.shape, F32)
    sub = iota((CO, SPAN), 1) % 4

    def coarse_back(t, c):
        block = cot_all[owner[0, 0, t], dest[0, 0, t]]
        wide = nn(block, spread[...])
        each = [jnp.where(sub == q, wide, 0.0).astype(BF16) for q in range(4)]
        flow_in[t] = nn(wb[...], jnp.concatenate(each, axis=0))
        gd[...] += nt(block, pt[t])
        return c

    for t in range(NT):
        coarse_back(t, 0)

    fold_rows, fold_cols = gds.shape[1], gds.shape[2]
    own_rows = CO // n2
    parts = fold_rows // own_rows
    natural = nt(gd[...].astype(BF16), perm[...])
    for k in range(n2):
        mine = natural[k * own_rows : (k + 1) * own_rows]
        gds[k] = jnp.concatenate(
            [mine[:, j * fold_cols : (j + 1) * fold_cols] for j in range(parts)], axis=0
        ).astype(BF16)

    def start_all(count, make):
        def go(d, c):
            make(d).start()
            return c

        lax.fori_loop(1, count, go, 0)

    def wait_all(count, make):
        def go(d, c):
            make(d).wait_recv()
            return c

        lax.fori_loop(1, count, go, 0)

    def sent_all(count, make):
        def go(d, c):
            make(d).wait_send()
            return c

        lax.fori_loop(1, count, go, 0)

    def scatter_copy(slot, src, dst):
        def make(d):
            to = lax.rem(k2 + d, n2)
            return remote(
                src(to), dst.at[d - 1], xy_ss.at[slot, d - 1], xy_rs.at[slot, d - 1], xy_device(d)
            )

        return make

    def z_copy(slot, src, dst):
        def make(d):
            return remote(src, dst.at[d - 1], z_ss.at[slot, d - 1], z_rs.at[slot, d - 1], z_device(d))

        return make

    def gather_copy(slot, buf):
        def make(d):
            return remote(
                buf.at[k2], buf.at[k2], xy_ss.at[slot, d - 1], xy_rs.at[slot, d - 1], xy_device(d)
            )

        return make

    big1 = scatter_copy(0, lambda to: gds.at[to], gdr)
    big2 = z_copy(0, gd2, gd2r)
    big3 = gather_copy(1, gd3)
    sm_rows = 4 * CH // n2
    small1 = scatter_copy(
        2, lambda to: sm1s.at[pl.ds(pl.multiple_of(to * sm_rows, sm_rows), sm_rows)], sm1r
    )
    small2 = z_copy(1, sm2, sm2r)
    small3 = gather_copy(3, sm3)

    def sum_slots(own, buf, count):
        def add(d, total):
            return total + buf[d].astype(F32)

        return lax.fori_loop(0, count, add, own)

    start_all(n2, big1)

    def big_second():
        wait_all(n2, big1)
        gd2[...] = sum_slots(gds[k2].astype(F32), gdr, n2 - 1)
        start_all(n1, big2)

    def big_third():
        wait_all(n1, big2)
        gd3[k2] = (sum_slots(gd2[...], gd2r, n1 - 1) * scale).astype(BF16)
        start_all(n2, big3)

    carry[...] = jnp.zeros(carry.shape, F32)
    dwacc[...] = jnp.zeros(dwacc.shape, F32)
    gkacc[...] = jnp.zeros(gkacc.shape, F32)

    def backward(n, c):
        t = NT - 1 - n
        for ic in range(4):
            ls = slice(ic * SPAN, (ic + 1) * SPAN)
            rows_in = [
                flow_in[t, p * CH : (p + 1) * CH, ic * NCOL : (ic + 1) * NCOL] for p in range(4)
            ]
            flow = carry[:, ls] + jnp.concatenate(rows_in, axis=1)
            act = flow * s_b[t, :, ls]
            dlt[0:CH, ls] = (flow * s_a[t, :, ls]).astype(BF16)
            dlt[CH : 2 * CH, ls] = (act * s_c[t, :, ls]).astype(BF16)
            dlt[2 * CH : 3 * CH, ls] = act.astype(BF16)
            dlt[3 * CH : 4 * CH, ls] = (act * s_r[t, :, ls]).astype(BF16)
            rev = nn(wall_t[...], dlt[:, ls])
            dcv[t, :, ls] = rev[0:CH].astype(BF16).astype(F32)
            carry[:, ls] = (1.0 - s_u[t, :, ls]) * flow + rev[CH : 2 * CH]
        dwacc[...] += nt(dlt[...], stk[t])

        def kernel_grad(g, c2):
            cs = chans(g)
            grads = [dcv[t, cs, i * NCOL : (i + 1) * NCOL] for i in range(NROW)]
            for tap in range(9):
                total = gkacc[tap, cs, :]
                for i in range(NROW):
                    total = total + grads[i] * xs[t, tap % 3, i + tap // 3, cs, :]
                gkacc[tap, cs, :] = total
            return c2

        lax.fori_loop(0, 4, kernel_grad, 0)
        if n == 2:
            big_second()
        return c

    for n in range(NT):
        backward(n, 0)

    lanes = iota((CH, NCOL), 1)
    sm1s[0 : 2 * CH, :] = dwacc[0 : 2 * CH, :]
    sm1s[2 * CH : 3 * CH, :] = jnp.where(
        lanes < CH, dwacc[2 * CH : 3 * CH, :], dwacc[3 * CH : 4 * CH, :]
    )
    columns = jnp.zeros((CH, NCOL), F32)
    for tap in range(9):
        columns = jnp.where(lanes == tap, jnp.sum(gkacc[tap], axis=1, keepdims=True), columns)
    sm1s[3 * CH : 4 * CH, :] = columns
    start_all(n2, small1)

    pack(1, dconv_row)
    halo1 = halo_copies(1)
    for copy in halo1:
        copy.start()

    for i in range(NROW):
        gstate[pl.ds(i, CH, stride=NROW), :] = carry[:, i * NCOL : (i + 1) * NCOL]

    wait_all(n2, small1)
    own = sm1s[pl.ds(pl.multiple_of(k2 * sm_rows, sm_rows), sm_rows), :]
    sm2[...] = sum_slots(own, sm1r, n2 - 1)
    start_all(n1, small2)

    for copy in key_copies + blk_copies:
        copy.wait_recv()

    def gather_blocks(n, c):
        at = pl.ds(pl.multiple_of(n * 32, 32), 32)
        totals = [jnp.zeros((32, NCOL), F32) for _ in range(NT)]
        for src in range(nr):
            for b in range(NT):
                key = key_all[src, b : b + 1, :]
                block = blk_all[src, b, at, :].astype(F32)
                for d in range(NT):
                    totals[d] = totals[d] + jnp.where(key == r * NT + d, block, 0.0)
        for d in range(NT):
            cart[d, at, :] = totals[d]
        return c

    lax.fori_loop(0, 4, gather_blocks, 0)
    big_third()

    wait_all(n1, small2)
    sm3[k2] = sum_slots(sm2[...], sm2r, n1 - 1) * scale
    start_all(n2, small3)

    for copy in halo1:
        copy.wait_recv()

    def conv_backward(n, c):
        t, g = n // 4, n % 4
        shifted = windows(1, dconv_row, t, g)

        def store(i, total):
            fx[pl.ds(t * NAT + g * GROUP * NROW + i, GROUP, stride=NROW), :] = total

        convolve(shifted, g, True, store)
        at = pl.ds(pl.multiple_of(n * 256, 256), 256)
        gfeat[at, :] = fx[at, :].astype(BF16)
        return c

    lax.fori_loop(0, 4 * NT, conv_backward, 0)

    wait_all(n2, big3)
    for k in range(n2):
        mine = gd3[k].astype(F32)
        for j in range(parts):
            gdown[k * own_rows : (k + 1) * own_rows, j * fold_cols : (j + 1) * fold_cols] = mine[
                j * own_rows : (j + 1) * own_rows
            ]

    wait_all(n2, small3)
    small = sm3[...].reshape(4 * CH, NCOL)
    ggate[...] = small[0 : 2 * CH]
    middle = small[2 * CH : 3 * CH]
    gcand[...] = middle[:, 0:CH]
    grecur[...] = pltpu.roll(middle, CH, 1)[:, 0:CH]
    lines = small[3 * CH : 4 * CH].T
    for tap in range(9):
        gkern[tap // 3, tap % 3 : tap % 3 + 1, :] = lines[tap : tap + 1, :]

    for copy in halo0 + halo1 + cot_copies + key_copies + blk_copies:
        copy.wait_send()
    sent_all(n2, big1)
    sent_all(n1, big2)
    sent_all(n2, big3)
    sent_all(n2, small1)
    sent_all(n1, small2)
    sent_all(n2, small3)


def publish(*refs):
    count = (len(refs) - 1) // 2
    copies = [
        pltpu.make_async_copy(refs[n], refs[count + n], refs[-1].at[n]) for n in range(count)
    ]
    for copy in copies:
        copy.start()
    for copy in copies:
        copy.wait()


def on_device(nr, na, *args):
    (features, state_init, kern, gate, cand, recur, down, owner_map, dest_map, cart_cot) = args
    scale = 1.0 / math.sqrt(NT * CELLS * nr * na)
    n2, n1 = na // 2, nr * 2
    own_rows = CO // n2
    parts = max(1, 16 // own_rows)
    fold = (own_rows * parts, 16 * CH // parts)
    sm_rows = 4 * CH // n2
    vmem = pl.BlockSpec(memory_space=pltpu.VMEM)
    smem = pl.BlockSpec(memory_space=pltpu.SMEM)
    hbm = pl.BlockSpec(memory_space=pltpu.HBM)
    dma = pltpu.SemaphoreType.DMA
    cells = (NT, CH, CELLS)
    scratch = [
        pltpu.VMEM((NT * NAT, NCOL), BF16),
        pltpu.VMEM((NAT, NCOL), BF16),
        pltpu.VMEM((3, 3, CH), F32),
        pltpu.VMEM((CH, CH), BF16),
        pltpu.VMEM((CH, CH), BF16),
        pltpu.VMEM((CO, 16 * CH), BF16),
        pltpu.VMEM((NT * NAT, NCOL), F32),
        pltpu.VMEM((NT, 3, NROW + 2, CH, NCOL), F32),
        pltpu.VMEM((NT, 2 * CH, CELLS), BF16),
        pltpu.VMEM((NT + 1, CH, CELLS), F32),
        pltpu.VMEM(cells, F32),
        pltpu.VMEM(cells, F32),
        pltpu.VMEM(cells, F32),
        pltpu.VMEM(cells, F32),
        pltpu.VMEM(cells, F32),
        pltpu.VMEM((NT, 4 * CH, SPAN), F32),
        pltpu.VMEM((NT, 16 * CH, 128), BF16),
        pltpu.VMEM((4 * CH, SPAN), BF16),
        pltpu.VMEM((1024, 1024), BF16),
        pltpu.VMEM((SPAN, SPAN), BF16),
        pltpu.VMEM((128, SPAN), BF16),
        pltpu.VMEM((4 * CH, 2 * CH), BF16),
        pltpu.VMEM((2 * CH, 4 * CH), BF16),
        pltpu.VMEM((CO, 16 * CH), BF16),
        pltpu.VMEM((4 * CH, 4 * CO), BF16),
        pltpu.VMEM((9, CH, NCOL), F32),
        pltpu.VMEM((4 * CH, CELLS), BF16),
        pltpu.VMEM(cells, F32),
        pltpu.VMEM((CH, CELLS), F32),
        pltpu.VMEM((4 * CH, 2 * CH), F32),
        pltpu.VMEM((9, CH, NCOL), F32),
        pltpu.VMEM((CO, 16 * CH), F32),
        pltpu.VMEM((2, 2, NT, CH, NCOL), BF16),
        pltpu.VMEM((2, 2, NT, CH, NCOL), BF16),
        pltpu.VMEM((2, 2, NT, CH, NCOL), BF16),
        pltpu.VMEM((2, 2, NT, CH, NCOL), BF16),
        pltpu.VMEM((2, CH, NCOL), BF16),
        pltpu.VMEM((2, 4, CH, NCOL), BF16),
        pltpu.VMEM((nr, NT, CO, 128), BF16),
        pltpu.VMEM((nr, 8, 128), I32),
        pltpu.VMEM((nr, NT, CO, 128), BF16),
        pltpu.VMEM((n2, *fold), BF16),
        pltpu.VMEM((n2 - 1, *fold), BF16),
        pltpu.VMEM(fold, F32),
        pltpu.VMEM((n1 - 1, *fold), F32),
        pltpu.VMEM((n2, *fold), BF16),
        pltpu.VMEM((4 * CH, NCOL), F32),
        pltpu.VMEM((n2 - 1, sm_rows, NCOL), F32),
        pltpu.VMEM((sm_rows, NCOL), F32),
        pltpu.VMEM((n1 - 1, sm_rows, NCOL), F32),
        pltpu.VMEM((n2, sm_rows, NCOL), F32),
        dma((8,)),
        dma((2, 8)),
        dma((2, 8)),
        dma((nr - 1,)),
        dma((nr - 1,)),
        dma((nr - 1,)),
        dma((nr - 1,)),
        dma((nr - 1,)),
        dma((nr - 1,)),
        dma((4, n2 - 1)),
        dma((4, n2 - 1)),
        dma((2, n1 - 1)),
        dma((2, n1 - 1)),
    ]
    results = (
        jax.ShapeDtypeStruct((NT, CO, 128), F32),
        jax.ShapeDtypeStruct((NT * NAT, NCOL), BF16),
        jax.ShapeDtypeStruct((NAT, NCOL), F32),
        jax.ShapeDtypeStruct((3, 3, CH), F32),
        jax.ShapeDtypeStruct((2 * CH, 2 * CH), F32),
        jax.ShapeDtypeStruct((CH, CH), F32),
        jax.ShapeDtypeStruct((CH, CH), F32),
        jax.ShapeDtypeStruct((CO, 16 * CH), F32),
    )
    out = pl.pallas_call(
        functools.partial(kernel, nr, na, scale),
        out_shape=tuple(pltpu.VMEM(x.shape, x.dtype) for x in results),
        in_specs=[hbm] * 7 + [smem] * 2 + [hbm],
        out_specs=(vmem,) * 8,
        scratch_shapes=scratch,
        compiler_params=pltpu.CompilerParams(
            collective_id=0, has_side_effects=True, vmem_limit_bytes=52 * 1024 * 1024
        ),
        name="section",
    )(
        features.reshape(NT * NAT, NCOL),
        state_init.reshape(NAT, NCOL),
        kern.transpose(1, 2, 0),
        gate,
        cand,
        recur,
        down,
        owner_map,
        dest_map,
        cart_cot.reshape(NT, CO, 128),
    )
    cart, gfeat, gstate, gkern, ggate, gcand, grecur, gdown = pl.pallas_call(
        publish,
        out_shape=results,
        in_specs=[vmem] * 8,
        out_specs=(pl.BlockSpec(memory_space=pl.ANY),) * 8,
        scratch_shapes=[dma((8,))],
        compiler_params=pltpu.CompilerParams(vmem_limit_bytes=1024 * 1024),
        name="publish",
    )(*(pltpu.with_memory_space_constraint(x, pltpu.VMEM) for x in out))
    return (
        cart.reshape(1, 1, NT, CO, 128),
        gfeat.reshape(NT, CH, NROW, NCOL),
        gstate.reshape(CH, NROW, NCOL),
        gkern.transpose(2, 0, 1),
        ggate,
        gcand,
        grecur,
        gdown,
    )


def solution(mesh):
    nr, na = mesh.shape["range"], mesh.shape["azimuth"]
    tile = P(None, "range", "azimuth")
    maps = P("range", "azimuth", None)
    cartesian = P("range", "azimuth", None, None, None)
    features = P(None, None, "range", "azimuth")
    return jax.shard_map(
        functools.partial(on_device, nr, na),
        mesh=mesh,
        in_specs=(features, tile, P(), P(), P(), P(), P(), maps, maps, cartesian),
        out_specs=(cartesian, features, tile, P(), P(), P(), P(), P()),
        check_vma=False,
    )
```

```python
import functools
import math

import jax
import jax.numpy as jnp
from jax import lax
from jax.experimental import pallas as pl
from jax.experimental.pallas import tpu as pltpu
from jax.sharding import PartitionSpec as P

MESH = pl.DeviceIdType.MESH
F32 = jnp.float32
BF16 = jnp.bfloat16
I32 = jnp.int32

CH = 64
NT = 4
NROW = 16
NCOL = 128
CELLS = NROW * NCOL
NAT = CH * NROW
CO = 128
SPAN = 512
GROUP = 16


def iota(shape, dim):
    return lax.broadcasted_iota(I32, shape, dim)


def nn(left, right):
    return lax.dot_general(left, right, (((1,), (0,)), ((), ())), preferred_element_type=F32)


def nt(left, right):
    return lax.dot_general(left, right, (((1,), (1,)), ((), ())), preferred_element_type=F32)


def remote(src, dst, send_sem, recv_sem, device):
    return pltpu.make_async_remote_copy(
        src_ref=src,
        dst_ref=dst,
        send_sem=send_sem,
        recv_sem=recv_sem,
        device_id=device,
        device_id_type=MESH,
    )


def kernel(
    nr,
    na,
    scale,
    feat_in,
    state_in,
    kern_in,
    gate_in,
    cand_in,
    recur_in,
    down_in,
    owner,
    dest,
    cot_in,
    cart,
    gfeat,
    gstate,
    gkern,
    ggate,
    gcand,
    grecur,
    gdown,
    feat,
    state,
    kern,
    cand,
    recur,
    down,
    fx,
    xs,
    stk,
    hs,
    s_a,
    s_b,
    s_c,
    s_r,
    s_u,
    flow_in,
    pt,
    hcat,
    perm,
    pick,
    spread,
    wall,
    wall_t,
    wp,
    wb,
    wk,
    dlt,
    dcv,
    carry,
    dwacc,
    gkacc,
    gd,
    row_s,
    row_r,
    col_s,
    col_r,
    cor_s,
    cor_r,
    cot_all,
    key_all,
    blk_all,
    gds,
    gdr,
    gd2,
    gd2r,
    gd3,
    sm1s,
    sm1r,
    sm2,
    sm2r,
    sm3,
    in_sem,
    halo_ss,
    halo_rs,
    cot_ss,
    cot_rs,
    key_ss,
    key_rs,
    blk_ss,
    blk_rs,
    xy_ss,
    xy_rs,
    z_ss,
    z_rs,
):
    r = lax.axis_index("range")
    a = lax.axis_index("azimuth")
    n2 = na // 2
    n1 = nr * 2
    k2 = a // 2
    zl = a % 2
    k1 = r * 2 + zl

    def ring_r(d):
        return lax.rem(r + d + nr, nr)

    def ring_a(d):
        return lax.rem(a + d + na, na)

    def xy_device(d):
        return (r, lax.rem(k2 + d, n2) * 2 + zl)

    def z_device(d):
        m = lax.rem(k1 + d, n1)
        return (m // 2, k2 * 2 + m % 2)

    barrier = pltpu.get_barrier_semaphore()

    def greet(device):
        pl.semaphore_signal(barrier, inc=1, device_id=device, device_id_type=MESH)

    diagonals = [(-1, -1), (-1, 1), (1, -1), (1, 1)]
    for da in (-1, 1):
        greet((r, ring_a(da)))
    for dr, da in diagonals:
        greet((ring_r(dr), ring_a(da)))

    for d in range(1, n2):
        greet(xy_device(d))
    for d in range(1, n1):
        greet(z_device(d))

    fetches = [
        pltpu.make_async_copy(src, dst, in_sem.at[n])
        for n, (src, dst) in enumerate(
            (
                (feat_in.at[pl.ds(0, NAT)], feat.at[pl.ds(0, NAT)]),
                (feat_in.at[pl.ds(NAT, (NT - 1) * NAT)], feat.at[pl.ds(NAT, (NT - 1) * NAT)]),
                (state_in, state),
                (kern_in, kern),
                (gate_in, wall.at[pl.ds(0, 2 * CH)]),
                (cand_in, cand),
                (recur_in, recur),
                (down_in, down),
                (cot_in, cot_all.at[r]),
            )
        )
    ]
    for fetch in fetches:
        fetch.start()

    lane = iota((GROUP, NCOL), 1)
    lane8 = lane // 8
    lane16 = lane // 16

    def chans(g):
        return pl.ds(pl.multiple_of(g * GROUP, GROUP), GROUP)

    def feature_row(t, g, i):
        return fx[pl.ds(t * NAT + g * GROUP * NROW + i, GROUP, stride=NROW), :]

    def dconv_row(t, g, i):
        return dcv[t, chans(g), pl.ds(i * NCOL, NCOL)]

    def pack(ph, batch, slices, row):
        def step(g, c):
            cs = chans(g)
            corner = jnp.zeros((GROUP, NCOL), F32)
            for t in slices:
                left = jnp.zeros((GROUP, NCOL), F32)
                right = jnp.zeros((GROUP, NCOL), F32)
                for i in range(NROW):
                    x = row(t, g, i)
                    y = pltpu.roll(x, 8 * i + 8, 1) if i < NROW - 1 else x
                    right = jnp.where(lane8 == i, y, right)
                    left = jnp.where(lane8 == (i + 1) % 16, y, left)
                    if i == 0:
                        row_s[ph, 0, t, cs, :] = x.astype(BF16)
                        y = pltpu.roll(x, 32 * t + 8, 1)
                        corner = jnp.where(lane16 == 2 * t, y, corner)
                    if i == NROW - 1:
                        row_s[ph, 1, t, cs, :] = x.astype(BF16)
                        y = pltpu.roll(x, (32 * t + 24) % NCOL, 1)
                        corner = jnp.where(lane16 == 2 * t + 1, y, corner)
                col_s[ph, 0, t, cs, :] = pltpu.roll(left, NCOL - 16, 1).astype(BF16)
                col_s[ph, 1, t, cs, :] = right.astype(BF16)
            cor_s[batch, cs, :] = corner.astype(BF16)
            return c

        lax.fori_loop(0, 4, step, 0)

    def halo_copies(ph, batch, first, count):
        copies = []
        some = pl.ds(first, count)
        for end, d in ((0, -1), (1, 1)):
            n = len(copies)
            copies.append(
                remote(
                    row_s.at[ph, end, some],
                    row_r.at[ph, 1 - end, some],
                    halo_ss.at[batch, n],
                    halo_rs.at[batch, n],
                    (ring_r(d), a),
                )
            )
        for end, d in ((0, -1), (1, 1)):
            n = len(copies)
            copies.append(
                remote(
                    col_s.at[ph, end, some],
                    col_r.at[ph, 1 - end, some],
                    halo_ss.at[batch, n],
                    halo_rs.at[batch, n],
                    (r, ring_a(d)),
                )
            )
        for j, (dr, da) in enumerate(diagonals):
            n = len(copies)
            copies.append(
                remote(
                    cor_s.at[batch],
                    cor_r.at[batch, 3 - j],
                    halo_ss.at[batch, n],
                    halo_rs.at[batch, n],
                    (ring_r(dr), ring_a(da)),
                )
            )
        return copies

    has_low = (r > 0).astype(F32)
    has_high = (r < nr - 1).astype(F32)

    def windows(ph, batch, row, t, g):
        cs = chans(g)
        halo_l = col_r[ph, 0, t, cs, :].astype(F32)
        halo_h = col_r[ph, 1, t, cs, :].astype(F32)
        out = [[None] * (NROW + 2) for _ in range(3)]

        def put(pos, x, low, high):
            out[0][pos] = jnp.where(lane < 8, low, pltpu.roll(x, 8, 1))
            out[1][pos] = x
            out[2][pos] = jnp.where(lane >= NCOL - 8, high, pltpu.roll(x, NCOL - 8, 1))

        for i in range(NROW):
            x = row(t, g, i)
            w = pltpu.roll(jnp.where(lane8 == i, halo_l, halo_h), (NCOL - 8 * i) % NCOL, 1)
            put(i + 1, x, w, w)
        for end in (0, 1):
            keep = has_low if end == 0 else has_high
            spot = 2 * t + (1 - end)
            x = row_r[ph, end, t, cs, :].astype(F32) * keep
            c_l = cor_r[batch, 2 * end, cs, :].astype(F32) * keep
            c_h = cor_r[batch, 2 * end + 1, cs, :].astype(F32) * keep
            low = pltpu.roll(c_l, lax.rem(NCOL - 16 * spot, NCOL), 1)
            high = pltpu.roll(c_h, 112 - 16 * spot, 1)
            put(0 if end == 0 else NROW + 1, x, low, high)
        return out

    def convolve(shifted, g, flipped, store):
        cs = chans(g)
        taps = [wk[8 - n if flipped else n, cs, :] for n in range(9)]
        for i in range(NROW):
            total = taps[0] * shifted[0][i]
            for n in range(1, 9):
                total = total + taps[n] * shifted[n % 3][i + n // 3]
            store(i, total)

    def widen(n, c):
        at = pl.ds(pl.multiple_of(n * 256, 256), 256)
        fx[at, :] = feat[at, :].astype(F32)
        return c

    key_row = iota((8, NCOL), 0)
    keys = jnp.zeros((8, NCOL), I32)
    for b in range(NT):
        keys = jnp.where(key_row == b, owner[0, 0, b] * NT + dest[0, 0, b], keys)
    key_all[r] = keys

    fetches[0].wait()
    lax.fori_loop(0, NAT // 256, widen, 0)
    pack(0, 0, [0], feature_row)
    pl.semaphore_wait(barrier, 6 + (n2 - 1) + (n1 - 1))
    first_halo = halo_copies(0, 0, 0, 1)
    for copy in first_halo:
        copy.start()
    fetches[1].wait()
    lax.fori_loop(NAT // 256, NT * NAT // 256, widen, 0)
    pack(0, 1, list(range(1, NT)), feature_row)
    rest_halo = halo_copies(0, 1, 1, NT - 1)
    for copy in rest_halo:
        copy.start()

    cot_copies = []
    key_copies = []
    for d in range(1, nr):
        device = (ring_r(d), a)
        key_copies.append(
            remote(key_all.at[r], key_all.at[r], key_ss.at[d - 1], key_rs.at[d - 1], device)
        )
        cot_copies.append(
            remote(cot_all.at[r], cot_all.at[r], cot_ss.at[d - 1], cot_rs.at[d - 1], device)
        )


    def make_perm(n, c):
        at = pl.multiple_of(n * 128, 128)
        src = iota((128, 1), 0) + at
        to = (src % 4) * 256 + ((src // 4) % 4) * CH + src // 16
        perm[pl.ds(at, 128), :] = (iota((128, 1024), 1) == to).astype(F32).astype(BF16)
        return c

    lax.fori_loop(0, 8, make_perm, 0)

    def make_pick(n, c):
        at = pl.multiple_of(n * 128, 128)
        src = iota((128, 1), 0) + at
        to = (src % 4) * 128 + (src // 128) * 32 + (src % 128) // 4
        pick[pl.ds(at, 128), :] = (iota((128, SPAN), 1) == to).astype(F32).astype(BF16)
        return c

    lax.fori_loop(0, 4, make_pick, 0)
    dst = iota((128, SPAN), 1)
    spread[...] = (iota((128, SPAN), 0) == (dst // 128) * 32 + (dst % 128) // 4).astype(F32).astype(BF16)

    place = iota((CH, 2 * CH), 1) - iota((CH, 2 * CH), 0)
    for fetch in fetches[2:]:
        fetch.wait()
    for copy in cot_copies + key_copies:
        copy.start()
    wall[2 * CH : 3 * CH, :] = nn(cand[...], (place == 0).astype(F32).astype(BF16)).astype(BF16)
    wall[3 * CH : 4 * CH, :] = nn(recur[...], (place == CH).astype(F32).astype(BF16)).astype(BF16)
    wall_t[...] = wall[...].astype(F32).T.astype(BF16)
    for q in range(4):
        part = nn(down[...], perm[:, q * 256 : (q + 1) * 256])
        wp[:, q * 256 : (q + 1) * 256] = part.astype(BF16)
        wb[:, q * 128 : (q + 1) * 128] = part.T.astype(BF16)
    for n in range(9):
        line = kern[n // 3, n % 3 : n % 3 + 1, :]
        wk[n] = jnp.broadcast_to(line, (NCOL, CH)).T
    gstate[...] = state[...].astype(F32)
    for i in range(NROW):
        hs[0, :, i * NCOL : (i + 1) * NCOL] = gstate[pl.ds(i, CH, stride=NROW), :]

    def conv_forward(batch, n, c):
        t, g = n // 4, n % 4
        cs = chans(g)
        shifted = windows(0, batch, feature_row, t, g)
        for b in range(3):
            for i in range(NROW + 2):
                xs[t, b, i, cs, :] = shifted[b][i]

        def store(i, total):
            stk[t, cs, i * NCOL : (i + 1) * NCOL] = total.astype(BF16)

        convolve(shifted, g, False, store)
        return c

    def forward(t, c):
        for ic in range(4):
            ls = slice(ic * SPAN, (ic + 1) * SPAN)
            h = hs[t, :, ls]
            stk[t, CH : 2 * CH, ls] = h.astype(BF16)
            pre = nn(wall[...], stk[t, :, ls])
            u = 0.5 * jnp.tanh(0.5 * pre[0:CH]) + 0.5
            z = 0.5 * jnp.tanh(0.5 * pre[CH : 2 * CH]) + 0.5
            rec = pre[3 * CH : 4 * CH]
            act = jnp.tanh(pre[2 * CH : 3 * CH] + z * rec)
            gap = act - h
            step = u * gap
            new = h + step
            hs[t + 1, :, ls] = new
            s_u[t, :, ls] = u
            s_r[t, :, ls] = z
            s_a[t, :, ls] = step * (1.0 - u)
            s_b[t, :, ls] = u * (1.0 - act * act)
            s_c[t, :, ls] = rec * z * (1.0 - z)
            new_bf = new.astype(BF16)
            for p in range(4):
                hcat[p * CH : (p + 1) * CH, ic * NCOL : (ic + 1) * NCOL] = new_bf[
                    :, p * NCOL : (p + 1) * NCOL
                ]
        sorted_lanes = nn(hcat[...], pick[...])
        for q in range(4):
            pt[t, q * 256 : (q + 1) * 256, :] = sorted_lanes[:, q * 128 : (q + 1) * 128].astype(BF16)
        blk_all[r, t] = nn(wp[...], pt[t]).astype(BF16)
        return c

    gd[...] = jnp.zeros(gd.shape, F32)
    sub = iota((CO, SPAN), 1) % 4

    def coarse_back(t, c):
        block = cot_all[owner[0, 0, t], dest[0, 0, t]]
        wide = nn(block, spread[...])
        each = [jnp.where(sub == q, wide, 0.0).astype(BF16) for q in range(4)]
        flow_in[t] = nn(wb[...], jnp.concatenate(each, axis=0))
        gd[...] += nt(block, pt[t])
        return c

    for copy in first_halo:
        copy.wait_recv()
    lax.fori_loop(0, 4, functools.partial(conv_forward, 0), 0)
    forward(0, 0)
    for copy in rest_halo:
        copy.wait_recv()
    lax.fori_loop(4, 4 * NT, functools.partial(conv_forward, 1), 0)
    for copy in cot_copies:
        copy.wait_recv()
    for t in range(1, NT):
        coarse_back(t - 1, 0)
        forward(t, 0)
    coarse_back(NT - 1, 0)

    blk_copies = []
    for d in range(1, nr):
        device = (ring_r(d), a)
        blk_copies.append(
            remote(blk_all.at[r], blk_all.at[r], blk_ss.at[d - 1], blk_rs.at[d - 1], device)
        )
    for copy in blk_copies:
        copy.start()

    fold_rows, fold_cols = gd2.shape
    own_rows = CO // n2
    parts = fold_rows // own_rows
    natural = nt(gd[...].astype(BF16), perm[...])
    for k in range(n2):
        mine = natural[k * own_rows : (k + 1) * own_rows]
        gds[k * fold_rows : (k + 1) * fold_rows] = jnp.concatenate(
            [mine[:, j * fold_cols : (j + 1) * fold_cols] for j in range(parts)], axis=0
        ).astype(BF16)

    def scatter(slot, src, piece, dst):
        def make(d):
            at = pl.ds(pl.multiple_of(lax.rem(k2 + d, n2) * piece, piece), piece)
            return remote(src.at[at], dst.at[d - 1], xy_ss.at[slot], xy_rs.at[slot], xy_device(d))

        every = remote(dst, dst, xy_ss.at[slot], xy_rs.at[slot], xy_device(1))
        return [make(d) for d in range(1, n2)], every

    def along_z(slot, src, dst):
        def make(d):
            return remote(src, dst.at[d - 1], z_ss.at[slot], z_rs.at[slot], z_device(d))

        every = remote(dst, dst, z_ss.at[slot], z_rs.at[slot], z_device(1))
        return [make(d) for d in range(1, n1)], every

    def gather(slot, buf):
        def make(d):
            return remote(buf.at[k2], buf.at[k2], xy_ss.at[slot], xy_rs.at[slot], xy_device(d))

        rest = buf.at[pl.ds(0, n2 - 1)]
        every = remote(rest, rest, xy_ss.at[slot], xy_rs.at[slot], xy_device(1))
        return [make(d) for d in range(1, n2)], every

    def start_all(exchange):
        for copy in exchange[0]:
            copy.start()

    def wait_all(exchange):
        exchange[1].wait_recv()

    def sent_all(exchange):
        exchange[1].wait_send()

    big1 = scatter(0, gds, fold_rows, gdr)
    big2 = along_z(0, gd2, gd2r)
    big3 = gather(1, gd3)
    sm_rows = 4 * CH // n2
    small1 = scatter(2, sm1s, sm_rows, sm1r)
    small2 = along_z(1, sm2, sm2r)
    small3 = gather(3, sm3)

    def sum_slots(own, buf, count):
        total = own
        for d in range(count):
            total = total + buf[d].astype(F32)
        return total

    start_all(big1)

    def big_second():
        wait_all(big1)
        own = gds[pl.ds(pl.multiple_of(k2 * fold_rows, fold_rows), fold_rows), :]
        gd2[...] = sum_slots(own.astype(F32), gdr, n2 - 1).astype(BF16)
        start_all(big2)

    def big_third():
        wait_all(big2)
        gd3[k2] = (sum_slots(gd2[...].astype(F32), gd2r, n1 - 1) * scale).astype(BF16)
        start_all(big3)

    carry[...] = jnp.zeros(carry.shape, F32)
    dwacc[...] = jnp.zeros(dwacc.shape, F32)
    gkacc[...] = jnp.zeros(gkacc.shape, F32)

    def backward(n, c):
        t = NT - 1 - n
        for ic in range(4):
            ls = slice(ic * SPAN, (ic + 1) * SPAN)
            rows_in = [
                flow_in[t, p * CH : (p + 1) * CH, ic * NCOL : (ic + 1) * NCOL] for p in range(4)
            ]
            flow = carry[:, ls] + jnp.concatenate(rows_in, axis=1)
            act = flow * s_b[t, :, ls]
            dlt[0:CH, ls] = (flow * s_a[t, :, ls]).astype(BF16)
            dlt[CH : 2 * CH, ls] = (act * s_c[t, :, ls]).astype(BF16)
            dlt[2 * CH : 3 * CH, ls] = act.astype(BF16)
            dlt[3 * CH : 4 * CH, ls] = (act * s_r[t, :, ls]).astype(BF16)
            rev = nn(wall_t[...], dlt[:, ls])
            dcv[t, :, ls] = rev[0:CH].astype(BF16).astype(F32)
            carry[:, ls] = (1.0 - s_u[t, :, ls]) * flow + rev[CH : 2 * CH]
        dwacc[...] += nt(dlt[...], stk[t])

        def kernel_grad(g, c2):
            cs = chans(g)
            grads = [dcv[t, cs, i * NCOL : (i + 1) * NCOL] for i in range(NROW)]
            for tap in range(9):
                total = gkacc[tap, cs, :]
                for i in range(NROW):
                    total = total + grads[i] * xs[t, tap % 3, i + tap // 3, cs, :]
                gkacc[tap, cs, :] = total
            return c2

        lax.fori_loop(0, 4, kernel_grad, 0)
        if n == 2:
            big_second()
        return c

    for n in range(NT):
        backward(n, 0)

    lanes = iota((CH, NCOL), 1)
    sm1s[0 : 2 * CH, :] = dwacc[0 : 2 * CH, :]
    sm1s[2 * CH : 3 * CH, :] = jnp.where(
        lanes < CH, dwacc[2 * CH : 3 * CH, :], dwacc[3 * CH : 4 * CH, :]
    )
    columns = jnp.zeros((CH, NCOL), F32)
    for tap in range(9):
        columns = jnp.where(lanes == tap, jnp.sum(gkacc[tap], axis=1, keepdims=True), columns)
    sm1s[3 * CH : 4 * CH, :] = columns
    start_all(small1)

    pack(1, 2, list(range(NT)), dconv_row)
    halo1 = halo_copies(1, 2, 0, NT)
    for copy in halo1:
        copy.start()

    for i in range(NROW):
        gstate[pl.ds(i, CH, stride=NROW), :] = carry[:, i * NCOL : (i + 1) * NCOL]

    wait_all(small1)
    own = sm1s[pl.ds(pl.multiple_of(k2 * sm_rows, sm_rows), sm_rows), :]
    sm2[...] = sum_slots(own, sm1r, n2 - 1)
    start_all(small2)

    for copy in key_copies + blk_copies:
        copy.wait_recv()

    def gather_blocks(n, c):
        at = pl.ds(pl.multiple_of(n * 32, 32), 32)
        totals = [jnp.zeros((32, NCOL), F32) for _ in range(NT)]
        for src in range(nr):
            for b in range(NT):
                key = key_all[src, b : b + 1, :]
                block = blk_all[src, b, at, :].astype(F32)
                for d in range(NT):
                    totals[d] = totals[d] + jnp.where(key == r * NT + d, block, 0.0)
        for d in range(NT):
            cart[d, at, :] = totals[d]
        return c

    lax.fori_loop(0, 4, gather_blocks, 0)
    big_third()

    wait_all(small2)
    sm3[k2] = sum_slots(sm2[...], sm2r, n1 - 1) * scale
    start_all(small3)

    for copy in halo1:
        copy.wait_recv()

    def conv_backward(n, c):
        t, g = n // 4, n % 4
        shifted = windows(1, 2, dconv_row, t, g)

        def store(i, total):
            fx[pl.ds(t * NAT + g * GROUP * NROW + i, GROUP, stride=NROW), :] = total

        convolve(shifted, g, True, store)
        at = pl.ds(pl.multiple_of(n * 256, 256), 256)
        gfeat[at, :] = fx[at, :].astype(BF16)
        return c

    lax.fori_loop(0, 4 * NT, conv_backward, 0)

    wait_all(big3)
    for k in range(n2):
        mine = gd3[k].astype(F32)
        for j in range(parts):
            gdown[k * own_rows : (k + 1) * own_rows, j * fold_cols : (j + 1) * fold_cols] = mine[
                j * own_rows : (j + 1) * own_rows
            ]

    wait_all(small3)
    small = sm3[...].reshape(4 * CH, NCOL)
    ggate[...] = small[0 : 2 * CH]
    middle = small[2 * CH : 3 * CH]
    gcand[...] = middle[:, 0:CH]
    grecur[...] = pltpu.roll(middle, CH, 1)[:, 0:CH]
    lines = small[3 * CH : 4 * CH].T
    for tap in range(9):
        gkern[tap // 3, tap % 3 : tap % 3 + 1, :] = lines[tap : tap + 1, :]

    for copy in first_halo + rest_halo + halo1 + cot_copies + key_copies + blk_copies:
        copy.wait_send()
    sent_all(big1)
    sent_all(big2)
    sent_all(big3)
    sent_all(small1)
    sent_all(small2)
    sent_all(small3)


def publish(*refs):
    count = (len(refs) - 1) // 2
    copies = [
        pltpu.make_async_copy(refs[n], refs[count + n], refs[-1].at[n]) for n in range(count)
    ]
    for copy in copies:
        copy.start()
    for copy in copies:
        copy.wait()


def on_device(nr, na, *args):
    (features, state_init, kern, gate, cand, recur, down, owner_map, dest_map, cart_cot) = args
    scale = 1.0 / math.sqrt(NT * CELLS * nr * na)
    n2, n1 = na // 2, nr * 2
    own_rows = CO // n2
    parts = max(1, 16 // own_rows)
    fold = (own_rows * parts, 16 * CH // parts)
    sm_rows = 4 * CH // n2
    vmem = pl.BlockSpec(memory_space=pltpu.VMEM)
    smem = pl.BlockSpec(memory_space=pltpu.SMEM)
    hbm = pl.BlockSpec(memory_space=pltpu.HBM)
    dma = pltpu.SemaphoreType.DMA
    cells = (NT, CH, CELLS)
    scratch = [
        pltpu.VMEM((NT * NAT, NCOL), BF16),
        pltpu.VMEM((NAT, NCOL), BF16),
        pltpu.VMEM((3, 3, CH), F32),
        pltpu.VMEM((CH, CH), BF16),
        pltpu.VMEM((CH, CH), BF16),
        pltpu.VMEM((CO, 16 * CH), BF16),
        pltpu.VMEM((NT * NAT, NCOL), F32),
        pltpu.VMEM((NT, 3, NROW + 2, CH, NCOL), F32),
        pltpu.VMEM((NT, 2 * CH, CELLS), BF16),
        pltpu.VMEM((NT + 1, CH, CELLS), F32),
        pltpu.VMEM(cells, F32),
        pltpu.VMEM(cells, F32),
        pltpu.VMEM(cells, F32),
        pltpu.VMEM(cells, F32),
        pltpu.VMEM(cells, F32),
        pltpu.VMEM((NT, 4 * CH, SPAN), F32),
        pltpu.VMEM((NT, 16 * CH, 128), BF16),
        pltpu.VMEM((4 * CH, SPAN), BF16),
        pltpu.VMEM((1024, 1024), BF16),
        pltpu.VMEM((SPAN, SPAN), BF16),
        pltpu.VMEM((128, SPAN), BF16),
        pltpu.VMEM((4 * CH, 2 * CH), BF16),
        pltpu.VMEM((2 * CH, 4 * CH), BF16),
        pltpu.VMEM((CO, 16 * CH), BF16),
        pltpu.VMEM((4 * CH, 4 * CO), BF16),
        pltpu.VMEM((9, CH, NCOL), F32),
        pltpu.VMEM((4 * CH, CELLS), BF16),
        pltpu.VMEM(cells, F32),
        pltpu.VMEM((CH, CELLS), F32),
        pltpu.VMEM((4 * CH, 2 * CH), F32),
        pltpu.VMEM((9, CH, NCOL), F32),
        pltpu.VMEM((CO, 16 * CH), F32),
        pltpu.VMEM((2, 2, NT, CH, NCOL), BF16),
        pltpu.VMEM((2, 2, NT, CH, NCOL), BF16),
        pltpu.VMEM((2, 2, NT, CH, NCOL), BF16),
        pltpu.VMEM((2, 2, NT, CH, NCOL), BF16),
        pltpu.VMEM((3, CH, NCOL), BF16),
        pltpu.VMEM((3, 4, CH, NCOL), BF16),
        pltpu.VMEM((nr, NT, CO, 128), BF16),
        pltpu.VMEM((nr, 8, 128), I32),
        pltpu.VMEM((nr, NT, CO, 128), BF16),
        pltpu.VMEM((n2 * fold[0], fold[1]), BF16),
        pltpu.VMEM((n2 - 1, *fold), BF16),
        pltpu.VMEM(fold, BF16),
        pltpu.VMEM((n1 - 1, *fold), BF16),
        pltpu.VMEM((n2, *fold), BF16),
        pltpu.VMEM((4 * CH, NCOL), F32),
        pltpu.VMEM((n2 - 1, sm_rows, NCOL), F32),
        pltpu.VMEM((sm_rows, NCOL), F32),
        pltpu.VMEM((n1 - 1, sm_rows, NCOL), F32),
        pltpu.VMEM((n2, sm_rows, NCOL), F32),
        dma((9,)),
        dma((3, 8)),
        dma((3, 8)),
        dma((nr - 1,)),
        dma((nr - 1,)),
        dma((nr - 1,)),
        dma((nr - 1,)),
        dma((nr - 1,)),
        dma((nr - 1,)),
        dma((4,)),
        dma((4,)),
        dma((2,)),
        dma((2,)),
    ]
    results = (
        jax.ShapeDtypeStruct((NT, CO, 128), F32),
        jax.ShapeDtypeStruct((NT * NAT, NCOL), BF16),
        jax.ShapeDtypeStruct((NAT, NCOL), F32),
        jax.ShapeDtypeStruct((3, 3, CH), F32),
        jax.ShapeDtypeStruct((2 * CH, 2 * CH), F32),
        jax.ShapeDtypeStruct((CH, CH), F32),
        jax.ShapeDtypeStruct((CH, CH), F32),
        jax.ShapeDtypeStruct((CO, 16 * CH), F32),
    )
    out = pl.pallas_call(
        functools.partial(kernel, nr, na, scale),
        out_shape=tuple(pltpu.VMEM(x.shape, x.dtype) for x in results),
        in_specs=[hbm] * 7 + [smem] * 2 + [hbm],
        out_specs=(vmem,) * 8,
        scratch_shapes=scratch,
        compiler_params=pltpu.CompilerParams(
            collective_id=0, has_side_effects=True, vmem_limit_bytes=52 * 1024 * 1024
        ),
        name="section",
    )(
        features.reshape(NT * NAT, NCOL),
        state_init.reshape(NAT, NCOL),
        kern.transpose(1, 2, 0),
        gate,
        cand,
        recur,
        down,
        owner_map,
        dest_map,
        cart_cot.reshape(NT, CO, 128),
    )
    cart, gfeat, gstate, gkern, ggate, gcand, grecur, gdown = pl.pallas_call(
        publish,
        out_shape=results,
        in_specs=[vmem] * 8,
        out_specs=(pl.BlockSpec(memory_space=pl.ANY),) * 8,
        scratch_shapes=[dma((8,))],
        compiler_params=pltpu.CompilerParams(vmem_limit_bytes=1024 * 1024),
        name="publish",
    )(*(pltpu.with_memory_space_constraint(x, pltpu.VMEM) for x in out))
    return (
        cart.reshape(1, 1, NT, CO, 128),
        gfeat.reshape(NT, CH, NROW, NCOL),
        gstate.reshape(CH, NROW, NCOL),
        gkern.transpose(2, 0, 1),
        ggate,
        gcand,
        grecur,
        gdown,
    )


def solution(mesh):
    nr, na = mesh.shape["range"], mesh.shape["azimuth"]
    tile = P(None, "range", "azimuth")
    maps = P("range", "azimuth", None)
    cartesian = P("range", "azimuth", None, None, None)
    features = P(None, None, "range", "azimuth")
    return jax.shard_map(
        functools.partial(on_device, nr, na),
        mesh=mesh,
        in_specs=(features, tile, P(), P(), P(), P(), P(), maps, maps, cartesian),
        out_specs=(cartesian, features, tile, P(), P(), P(), P(), P()),
        check_vma=False,
    )
```

```python
import functools
import math

import jax
import jax.numpy as jnp
from jax import lax
from jax.experimental import pallas as pl
from jax.experimental.pallas import tpu as pltpu
from jax.sharding import PartitionSpec as P

MESH = pl.DeviceIdType.MESH
F32 = jnp.float32
BF16 = jnp.bfloat16
I32 = jnp.int32

CH = 64
NT = 4
NROW = 16
NCOL = 128
CELLS = NROW * NCOL
NAT = CH * NROW
CO = 128
SPAN = 512
GROUP = 16


def iota(shape, dim):
    return lax.broadcasted_iota(I32, shape, dim)


def nn(left, right):
    return lax.dot_general(left, right, (((1,), (0,)), ((), ())), preferred_element_type=F32)


def nt(left, right):
    return lax.dot_general(left, right, (((1,), (1,)), ((), ())), preferred_element_type=F32)


def remote(src, dst, send_sem, recv_sem, device):
    return pltpu.make_async_remote_copy(
        src_ref=src,
        dst_ref=dst,
        send_sem=send_sem,
        recv_sem=recv_sem,
        device_id=device,
        device_id_type=MESH,
    )


def kernel(
    nr,
    na,
    scale,
    feat_in,
    state_in,
    kern_in,
    gate_in,
    cand_in,
    recur_in,
    down_in,
    owner,
    dest,
    cot_in,
    cart,
    gfeat,
    gstate,
    gkern,
    ggate,
    gcand,
    grecur,
    gdown,
    feat,
    state,
    kern,
    cand,
    recur,
    down,
    fx,
    xs,
    stk,
    hs,
    s_a,
    s_b,
    s_c,
    s_r,
    s_u,
    flow_in,
    pt,
    hcat,
    perm,
    pick,
    spread,
    wall,
    wall_t,
    wp,
    wb,
    wk,
    dlt,
    dcv,
    carry,
    dwacc,
    gkacc,
    gd,
    row_s,
    row_r,
    col_s,
    col_r,
    cor_s,
    cor_r,
    cot_all,
    key_all,
    blk_all,
    gds,
    gdr,
    gd2,
    gd2r,
    gd3,
    sm1s,
    sm1r,
    sm2,
    sm2r,
    sm3,
    in_sem,
    halo_ss,
    halo_rs,
    cot_ss,
    cot_rs,
    key_ss,
    key_rs,
    blk_ss,
    blk_rs,
    xy_ss,
    xy_rs,
    z_ss,
    z_rs,
):
    r = lax.axis_index("range")
    a = lax.axis_index("azimuth")
    n2 = na // 2
    n1 = nr * 2
    k2 = a // 2
    zl = a % 2
    k1 = r * 2 + zl

    def ring_r(d):
        return lax.rem(r + d + nr, nr)

    def ring_a(d):
        return lax.rem(a + d + na, na)

    def xy_device(d):
        return (r, lax.rem(k2 + d, n2) * 2 + zl)

    def z_device(d):
        m = lax.rem(k1 + d, n1)
        return (m // 2, k2 * 2 + m % 2)

    barrier = pltpu.get_barrier_semaphore()

    def greet(device):
        pl.semaphore_signal(barrier, inc=1, device_id=device, device_id_type=MESH)

    diagonals = [(-1, -1), (-1, 1), (1, -1), (1, 1)]
    for da in (-1, 1):
        greet((r, ring_a(da)))
    for dr, da in diagonals:
        greet((ring_r(dr), ring_a(da)))

    for d in range(1, n2):
        greet(xy_device(d))
    for d in range(1, n1):
        greet(z_device(d))

    fetches = [
        pltpu.make_async_copy(src, dst, in_sem.at[n])
        for n, (src, dst) in enumerate(
            (
                (feat_in.at[pl.ds(0, NAT)], feat.at[pl.ds(0, NAT)]),
                (feat_in.at[pl.ds(NAT, (NT - 1) * NAT)], feat.at[pl.ds(NAT, (NT - 1) * NAT)]),
                (state_in, state),
                (kern_in, kern),
                (gate_in, wall.at[pl.ds(0, 2 * CH)]),
                (cand_in, cand),
                (recur_in, recur),
                (down_in, down),
                (cot_in, cot_all.at[r]),
            )
        )
    ]
    for fetch in fetches:
        fetch.start()

    lane = iota((GROUP, NCOL), 1)
    lane8 = lane // 8
    lane16 = lane // 16

    def chans(g):
        if isinstance(g, int):
            return pl.ds(g * GROUP, GROUP)
        return pl.ds(pl.multiple_of(g * GROUP, GROUP), GROUP)

    def feature_row(t, g, i):
        return fx[pl.ds(t * NAT + g * GROUP * NROW + i, GROUP, stride=NROW), :]

    def dconv_row(t, g, i):
        return dcv[t, chans(g), pl.ds(i * NCOL, NCOL)]

    def pack(ph, batch, slices, row):
        def step(g, c):
            cs = chans(g)
            corner = jnp.zeros((GROUP, NCOL), F32)
            for t in slices:
                left = jnp.zeros((GROUP, NCOL), F32)
                right = jnp.zeros((GROUP, NCOL), F32)
                for i in range(NROW):
                    x = row(t, g, i)
                    y = pltpu.roll(x, 8 * i + 8, 1) if i < NROW - 1 else x
                    right = jnp.where(lane8 == i, y, right)
                    left = jnp.where(lane8 == (i + 1) % 16, y, left)
                    if i == 0:
                        row_s[ph, 0, t, cs, :] = x.astype(BF16)
                        y = pltpu.roll(x, 32 * t + 8, 1)
                        corner = jnp.where(lane16 == 2 * t, y, corner)
                    if i == NROW - 1:
                        row_s[ph, 1, t, cs, :] = x.astype(BF16)
                        y = pltpu.roll(x, (32 * t + 24) % NCOL, 1)
                        corner = jnp.where(lane16 == 2 * t + 1, y, corner)
                col_s[ph, 0, t, cs, :] = pltpu.roll(left, NCOL - 16, 1).astype(BF16)
                col_s[ph, 1, t, cs, :] = right.astype(BF16)
            cor_s[batch, cs, :] = corner.astype(BF16)
            return c

        lax.fori_loop(0, 4, step, 0)

    def halo_copies(ph, batch, first, count):
        copies = []
        some = pl.ds(first, count)
        for end, d in ((0, -1), (1, 1)):
            n = len(copies)
            copies.append(
                remote(
                    row_s.at[ph, end, some],
                    row_r.at[ph, 1 - end, some],
                    halo_ss.at[batch, n],
                    halo_rs.at[batch, n],
                    (ring_r(d), a),
                )
            )
        for end, d in ((0, -1), (1, 1)):
            n = len(copies)
            copies.append(
                remote(
                    col_s.at[ph, end, some],
                    col_r.at[ph, 1 - end, some],
                    halo_ss.at[batch, n],
                    halo_rs.at[batch, n],
                    (r, ring_a(d)),
                )
            )
        for j, (dr, da) in enumerate(diagonals):
            n = len(copies)
            copies.append(
                remote(
                    cor_s.at[batch],
                    cor_r.at[batch, 3 - j],
                    halo_ss.at[batch, n],
                    halo_rs.at[batch, n],
                    (ring_r(dr), ring_a(da)),
                )
            )
        return copies

    has_low = (r > 0).astype(F32)
    has_high = (r < nr - 1).astype(F32)

    def windows(ph, batch, row, t, g):
        cs = chans(g)
        halo_l = col_r[ph, 0, t, cs, :].astype(F32)
        halo_h = col_r[ph, 1, t, cs, :].astype(F32)
        out = [[None] * (NROW + 2) for _ in range(3)]

        def put(pos, x, low, high):
            out[0][pos] = jnp.where(lane < 8, low, pltpu.roll(x, 8, 1))
            out[1][pos] = x
            out[2][pos] = jnp.where(lane >= NCOL - 8, high, pltpu.roll(x, NCOL - 8, 1))

        for i in range(NROW):
            x = row(t, g, i)
            w = pltpu.roll(jnp.where(lane8 == i, halo_l, halo_h), (NCOL - 8 * i) % NCOL, 1)
            put(i + 1, x, w, w)
        for end in (0, 1):
            keep = has_low if end == 0 else has_high
            spot = 2 * t + (1 - end)
            x = row_r[ph, end, t, cs, :].astype(F32) * keep
            c_l = cor_r[batch, 2 * end, cs, :].astype(F32) * keep
            c_h = cor_r[batch, 2 * end + 1, cs, :].astype(F32) * keep
            low = pltpu.roll(c_l, lax.rem(NCOL - 16 * spot, NCOL), 1)
            high = pltpu.roll(c_h, 112 - 16 * spot, 1)
            put(0 if end == 0 else NROW + 1, x, low, high)
        return out

    def convolve(shifted, g, flipped, store):
        cs = chans(g)
        taps = [wk[8 - n if flipped else n, cs, :] for n in range(9)]
        for i in range(NROW):
            total = taps[0] * shifted[0][i]
            for n in range(1, 9):
                total = total + taps[n] * shifted[n % 3][i + n // 3]
            store(i, total)

    def widen(n, c):
        at = pl.ds(pl.multiple_of(n * 256, 256), 256)
        fx[at, :] = feat[at, :].astype(F32)
        return c

    key_row = iota((8, NCOL), 0)
    keys = jnp.zeros((8, NCOL), I32)
    for b in range(NT):
        keys = jnp.where(key_row == b, owner[0, 0, b] * NT + dest[0, 0, b], keys)
    key_all[r] = keys

    fetches[0].wait()
    lax.fori_loop(0, NAT // 256, widen, 0)
    pack(0, 0, [0], feature_row)
    pl.semaphore_wait(barrier, 6 + (n2 - 1) + (n1 - 1))
    first_halo = halo_copies(0, 0, 0, 1)
    for copy in first_halo:
        copy.start()
    fetches[1].wait()
    lax.fori_loop(NAT // 256, NT * NAT // 256, widen, 0)
    pack(0, 1, list(range(1, NT)), feature_row)
    rest_halo = halo_copies(0, 1, 1, NT - 1)
    for copy in rest_halo:
        copy.start()

    cot_copies = []
    key_copies = []
    for d in range(1, nr):
        device = (ring_r(d), a)
        key_copies.append(
            remote(key_all.at[r], key_all.at[r], key_ss.at[d - 1], key_rs.at[d - 1], device)
        )
        cot_copies.append(
            remote(cot_all.at[r], cot_all.at[r], cot_ss.at[d - 1], cot_rs.at[d - 1], device)
        )

    fetches[-1].wait()
    for copy in cot_copies + key_copies:
        copy.start()


    def make_perm(n, c):
        at = pl.multiple_of(n * 128, 128)
        src = iota((128, 1), 0) + at
        to = (src % 4) * 256 + ((src // 4) % 4) * CH + src // 16
        perm[pl.ds(at, 128), :] = (iota((128, 1024), 1) == to).astype(F32).astype(BF16)
        return c

    lax.fori_loop(0, 8, make_perm, 0)

    def make_pick(n, c):
        at = pl.multiple_of(n * 128, 128)
        src = iota((128, 1), 0) + at
        to = (src % 4) * 128 + (src // 128) * 32 + (src % 128) // 4
        pick[pl.ds(at, 128), :] = (iota((128, SPAN), 1) == to).astype(F32).astype(BF16)
        return c

    lax.fori_loop(0, 4, make_pick, 0)
    dst = iota((128, SPAN), 1)
    spread[...] = (iota((128, SPAN), 0) == (dst // 128) * 32 + (dst % 128) // 4).astype(F32).astype(BF16)

    place = iota((CH, 2 * CH), 1) - iota((CH, 2 * CH), 0)
    for fetch in fetches[2:-1]:
        fetch.wait()
    wall[2 * CH : 3 * CH, :] = nn(cand[...], (place == 0).astype(F32).astype(BF16)).astype(BF16)
    wall[3 * CH : 4 * CH, :] = nn(recur[...], (place == CH).astype(F32).astype(BF16)).astype(BF16)
    wall_t[...] = wall[...].astype(F32).T.astype(BF16)
    for q in range(4):
        part = nn(down[...], perm[:, q * 256 : (q + 1) * 256])
        wp[:, q * 256 : (q + 1) * 256] = part.astype(BF16)
        wb[:, q * 128 : (q + 1) * 128] = part.T.astype(BF16)
    for n in range(9):
        line = kern[n // 3, n % 3 : n % 3 + 1, :]
        wk[n] = jnp.broadcast_to(line, (NCOL, CH)).T
    gstate[...] = state[...].astype(F32)
    for i in range(NROW):
        hs[0, :, i * NCOL : (i + 1) * NCOL] = gstate[pl.ds(i, CH, stride=NROW), :]

    def conv_forward(batch, n, c):
        t, g = n // 4, n % 4
        cs = chans(g)
        shifted = windows(0, batch, feature_row, t, g)
        for b in range(3):
            for i in range(NROW + 2):
                xs[t, b, i, cs, :] = shifted[b][i]

        def store(i, total):
            stk[t, cs, i * NCOL : (i + 1) * NCOL] = total.astype(BF16)

        convolve(shifted, g, False, store)
        return c

    def forward(t, c):
        for ic in range(4):
            ls = slice(ic * SPAN, (ic + 1) * SPAN)
            h = hs[t, :, ls]
            stk[t, CH : 2 * CH, ls] = h.astype(BF16)
            pre = nn(wall[...], stk[t, :, ls])
            u = 0.5 * jnp.tanh(0.5 * pre[0:CH]) + 0.5
            z = 0.5 * jnp.tanh(0.5 * pre[CH : 2 * CH]) + 0.5
            rec = pre[3 * CH : 4 * CH]
            act = jnp.tanh(pre[2 * CH : 3 * CH] + z * rec)
            gap = act - h
            step = u * gap
            new = h + step
            hs[t + 1, :, ls] = new
            s_u[t, :, ls] = u
            s_r[t, :, ls] = z
            s_a[t, :, ls] = step * (1.0 - u)
            s_b[t, :, ls] = u * (1.0 - act * act)
            s_c[t, :, ls] = rec * z * (1.0 - z)
            new_bf = new.astype(BF16)
            for p in range(4):
                hcat[p * CH : (p + 1) * CH, ic * NCOL : (ic + 1) * NCOL] = new_bf[
                    :, p * NCOL : (p + 1) * NCOL
                ]
        sorted_lanes = nn(hcat[...], pick[...])
        for q in range(4):
            pt[t, q * 256 : (q + 1) * 256, :] = sorted_lanes[:, q * 128 : (q + 1) * 128].astype(BF16)
        blk_all[r, t] = nn(wp[...], pt[t]).astype(BF16)
        return c

    gd[...] = jnp.zeros(gd.shape, F32)
    sub = iota((CO, SPAN), 1) % 4

    def coarse_back(t, c):
        block = cot_all[owner[0, 0, t], dest[0, 0, t]]
        wide = nn(block, spread[...])
        each = [jnp.where(sub == q, wide, 0.0).astype(BF16) for q in range(4)]
        flow_in[t] = nn(wb[...], jnp.concatenate(each, axis=0))
        gd[...] += nt(block, pt[t])
        return c

    for copy in first_halo:
        copy.wait_recv()
    lax.fori_loop(0, 4, functools.partial(conv_forward, 0), 0)
    forward(0, 0)
    for copy in rest_halo:
        copy.wait_recv()
    lax.fori_loop(4, 4 * NT, functools.partial(conv_forward, 1), 0)
    for t in range(1, NT - 1):
        forward(t, 0)
    for copy in cot_copies:
        copy.wait_recv()
    coarse_back(0, 0)
    forward(NT - 1, 0)
    for t in range(1, NT):
        coarse_back(t, 0)

    blk_copies = []
    for d in range(1, nr):
        device = (ring_r(d), a)
        blk_copies.append(
            remote(blk_all.at[r], blk_all.at[r], blk_ss.at[d - 1], blk_rs.at[d - 1], device)
        )
    for copy in blk_copies:
        copy.start()

    fold_rows, fold_cols = gd2.shape
    own_rows = CO // n2
    parts = fold_rows // own_rows
    natural = nt(gd[...].astype(BF16), perm[...])
    for k in range(n2):
        mine = natural[k * own_rows : (k + 1) * own_rows]
        gds[k * fold_rows : (k + 1) * fold_rows] = jnp.concatenate(
            [mine[:, j * fold_cols : (j + 1) * fold_cols] for j in range(parts)], axis=0
        ).astype(BF16)

    def scatter(slot, src, piece, dst):
        def make(d):
            at = pl.ds(pl.multiple_of(lax.rem(k2 + d, n2) * piece, piece), piece)
            return remote(src.at[at], dst.at[d - 1], xy_ss.at[slot], xy_rs.at[slot], xy_device(d))

        every = remote(dst, dst, xy_ss.at[slot], xy_rs.at[slot], xy_device(1))
        return [make(d) for d in range(1, n2)], every

    def along_z(slot, src, dst):
        def make(d):
            return remote(src, dst.at[d - 1], z_ss.at[slot], z_rs.at[slot], z_device(d))

        every = remote(dst, dst, z_ss.at[slot], z_rs.at[slot], z_device(1))
        return [make(d) for d in range(1, n1)], every

    def gather(slot, buf):
        def make(d):
            return remote(buf.at[k2], buf.at[k2], xy_ss.at[slot], xy_rs.at[slot], xy_device(d))

        rest = buf.at[pl.ds(0, n2 - 1)]
        every = remote(rest, rest, xy_ss.at[slot], xy_rs.at[slot], xy_device(1))
        return [make(d) for d in range(1, n2)], every

    def start_all(exchange):
        for copy in exchange[0]:
            copy.start()

    def wait_all(exchange):
        exchange[1].wait_recv()

    def sent_all(exchange):
        exchange[1].wait_send()

    big1 = scatter(0, gds, fold_rows, gdr)
    big2 = along_z(0, gd2, gd2r)
    big3 = gather(1, gd3)
    sm_rows = 4 * CH // n2
    small1 = scatter(2, sm1s, sm_rows, sm1r)
    small2 = along_z(1, sm2, sm2r)
    small3 = gather(3, sm3)

    def sum_slots(own, buf, count):
        total = own
        for d in range(count):
            total = total + buf[d].astype(F32)
        return total

    start_all(big1)

    def big_second():
        wait_all(big1)
        own = gds[pl.ds(pl.multiple_of(k2 * fold_rows, fold_rows), fold_rows), :]
        gd2[...] = sum_slots(own.astype(F32), gdr, n2 - 1).astype(BF16)
        start_all(big2)

    def big_third():
        wait_all(big2)
        gd3[k2] = (sum_slots(gd2[...].astype(F32), gd2r, n1 - 1) * scale).astype(BF16)
        start_all(big3)

    carry[...] = jnp.zeros(carry.shape, F32)
    dwacc[...] = jnp.zeros(dwacc.shape, F32)
    gkacc[...] = jnp.zeros(gkacc.shape, F32)

    def backward(n, c):
        t = NT - 1 - n
        for ic in range(4):
            ls = slice(ic * SPAN, (ic + 1) * SPAN)
            rows_in = [
                flow_in[t, p * CH : (p + 1) * CH, ic * NCOL : (ic + 1) * NCOL] for p in range(4)
            ]
            flow = carry[:, ls] + jnp.concatenate(rows_in, axis=1)
            act = flow * s_b[t, :, ls]
            dlt[0:CH, ls] = (flow * s_a[t, :, ls]).astype(BF16)
            dlt[CH : 2 * CH, ls] = (act * s_c[t, :, ls]).astype(BF16)
            dlt[2 * CH : 3 * CH, ls] = act.astype(BF16)
            dlt[3 * CH : 4 * CH, ls] = (act * s_r[t, :, ls]).astype(BF16)
            rev = nn(wall_t[...], dlt[:, ls])
            dcv[t, :, ls] = rev[0:CH].astype(BF16).astype(F32)
            carry[:, ls] = (1.0 - s_u[t, :, ls]) * flow + rev[CH : 2 * CH]
        dwacc[...] += nt(dlt[...], stk[t])

        def kernel_grad(g, c2):
            cs = chans(g)
            grads = [dcv[t, cs, i * NCOL : (i + 1) * NCOL] for i in range(NROW)]
            for tap in range(9):
                total = gkacc[tap, cs, :]
                for i in range(NROW):
                    total = total + grads[i] * xs[t, tap % 3, i + tap // 3, cs, :]
                gkacc[tap, cs, :] = total
            return c2

        for g in range(4):
            kernel_grad(g, 0)
        if n == 3:
            big_second()
        return c

    for n in range(NT):
        backward(n, 0)

    lanes = iota((CH, NCOL), 1)
    sm1s[0 : 2 * CH, :] = dwacc[0 : 2 * CH, :]
    sm1s[2 * CH : 3 * CH, :] = jnp.where(
        lanes < CH, dwacc[2 * CH : 3 * CH, :], dwacc[3 * CH : 4 * CH, :]
    )
    columns = jnp.zeros((CH, NCOL), F32)
    for tap in range(9):
        columns = jnp.where(lanes == tap, jnp.sum(gkacc[tap], axis=1, keepdims=True), columns)
    sm1s[3 * CH : 4 * CH, :] = columns
    start_all(small1)

    pack(1, 2, list(range(NT)), dconv_row)
    halo1 = halo_copies(1, 2, 0, NT)
    for copy in halo1:
        copy.start()

    for i in range(NROW):
        gstate[pl.ds(i, CH, stride=NROW), :] = carry[:, i * NCOL : (i + 1) * NCOL]

    wait_all(small1)
    own = sm1s[pl.ds(pl.multiple_of(k2 * sm_rows, sm_rows), sm_rows), :]
    sm2[...] = sum_slots(own, sm1r, n2 - 1)
    start_all(small2)

    for copy in key_copies + blk_copies:
        copy.wait_recv()

    def gather_blocks(n, c):
        at = pl.ds(pl.multiple_of(n * 32, 32), 32)
        totals = [jnp.zeros((32, NCOL), F32) for _ in range(NT)]
        for src in range(nr):
            for b in range(NT):
                key = key_all[src, b : b + 1, :]
                block = blk_all[src, b, at, :].astype(F32)
                for d in range(NT):
                    totals[d] = totals[d] + jnp.where(key == r * NT + d, block, 0.0)
        for d in range(NT):
            cart[d, at, :] = totals[d]
        return c

    lax.fori_loop(0, 4, gather_blocks, 0)
    big_third()

    wait_all(small2)
    sm3[k2] = sum_slots(sm2[...], sm2r, n1 - 1) * scale
    start_all(small3)

    for copy in halo1:
        copy.wait_recv()

    def conv_backward(n, c):
        t, g = n // 4, n % 4
        shifted = windows(1, 2, dconv_row, t, g)

        def store(i, total):
            fx[pl.ds(t * NAT + g * GROUP * NROW + i, GROUP, stride=NROW), :] = total

        convolve(shifted, g, True, store)
        at = pl.ds(pl.multiple_of(n * 256, 256), 256)
        gfeat[at, :] = fx[at, :].astype(BF16)
        return c

    lax.fori_loop(0, 4 * NT, conv_backward, 0)

    wait_all(big3)
    for k in range(n2):
        mine = gd3[k].astype(F32)
        for j in range(parts):
            gdown[k * own_rows : (k + 1) * own_rows, j * fold_cols : (j + 1) * fold_cols] = mine[
                j * own_rows : (j + 1) * own_rows
            ]

    wait_all(small3)
    small = sm3[...].reshape(4 * CH, NCOL)
    ggate[...] = small[0 : 2 * CH]
    middle = small[2 * CH : 3 * CH]
    gcand[...] = middle[:, 0:CH]
    grecur[...] = pltpu.roll(middle, CH, 1)[:, 0:CH]
    lines = small[3 * CH : 4 * CH].T
    for tap in range(9):
        gkern[tap // 3, tap % 3 : tap % 3 + 1, :] = lines[tap : tap + 1, :]

    for copy in first_halo + rest_halo + halo1 + cot_copies + key_copies + blk_copies:
        copy.wait_send()
    sent_all(big1)
    sent_all(big2)
    sent_all(big3)
    sent_all(small1)
    sent_all(small2)
    sent_all(small3)


def publish(*refs):
    count = (len(refs) - 1) // 2
    copies = [
        pltpu.make_async_copy(refs[n], refs[count + n], refs[-1].at[n]) for n in range(count)
    ]
    for copy in copies:
        copy.start()
    for copy in copies:
        copy.wait()


def on_device(nr, na, *args):
    (features, state_init, kern, gate, cand, recur, down, owner_map, dest_map, cart_cot) = args
    scale = 1.0 / math.sqrt(NT * CELLS * nr * na)
    n2, n1 = na // 2, nr * 2
    own_rows = CO // n2
    parts = max(1, 16 // own_rows)
    fold = (own_rows * parts, 16 * CH // parts)
    sm_rows = 4 * CH // n2
    vmem = pl.BlockSpec(memory_space=pltpu.VMEM)
    smem = pl.BlockSpec(memory_space=pltpu.SMEM)
    hbm = pl.BlockSpec(memory_space=pltpu.HBM)
    dma = pltpu.SemaphoreType.DMA
    cells = (NT, CH, CELLS)
    scratch = [
        pltpu.VMEM((NT * NAT, NCOL), BF16),
        pltpu.VMEM((NAT, NCOL), BF16),
        pltpu.VMEM((3, 3, CH), F32),
        pltpu.VMEM((CH, CH), BF16),
        pltpu.VMEM((CH, CH), BF16),
        pltpu.VMEM((CO, 16 * CH), BF16),
        pltpu.VMEM((NT * NAT, NCOL), F32),
        pltpu.VMEM((NT, 3, NROW + 2, CH, NCOL), F32),
        pltpu.VMEM((NT, 2 * CH, CELLS), BF16),
        pltpu.VMEM((NT + 1, CH, CELLS), F32),
        pltpu.VMEM(cells, F32),
        pltpu.VMEM(cells, F32),
        pltpu.VMEM(cells, F32),
        pltpu.VMEM(cells, F32),
        pltpu.VMEM(cells, F32),
        pltpu.VMEM((NT, 4 * CH, SPAN), F32),
        pltpu.VMEM((NT, 16 * CH, 128), BF16),
        pltpu.VMEM((4 * CH, SPAN), BF16),
        pltpu.VMEM((1024, 1024), BF16),
        pltpu.VMEM((SPAN, SPAN), BF16),
        pltpu.VMEM((128, SPAN), BF16),
        pltpu.VMEM((4 * CH, 2 * CH), BF16),
        pltpu.VMEM((2 * CH, 4 * CH), BF16),
        pltpu.VMEM((CO, 16 * CH), BF16),
        pltpu.VMEM((4 * CH, 4 * CO), BF16),
        pltpu.VMEM((9, CH, NCOL), F32),
        pltpu.VMEM((4 * CH, CELLS), BF16),
        pltpu.VMEM(cells, F32),
        pltpu.VMEM((CH, CELLS), F32),
        pltpu.VMEM((4 * CH, 2 * CH), F32),
        pltpu.VMEM((9, CH, NCOL), F32),
        pltpu.VMEM((CO, 16 * CH), F32),
        pltpu.VMEM((2, 2, NT, CH, NCOL), BF16),
        pltpu.VMEM((2, 2, NT, CH, NCOL), BF16),
        pltpu.VMEM((2, 2, NT, CH, NCOL), BF16),
        pltpu.VMEM((2, 2, NT, CH, NCOL), BF16),
        pltpu.VMEM((3, CH, NCOL), BF16),
        pltpu.VMEM((3, 4, CH, NCOL), BF16),
        pltpu.VMEM((nr, NT, CO, 128), BF16),
        pltpu.VMEM((nr, 8, 128), I32),
        pltpu.VMEM((nr, NT, CO, 128), BF16),
        pltpu.VMEM((n2 * fold[0], fold[1]), BF16),
        pltpu.VMEM((n2 - 1, *fold), BF16),
        pltpu.VMEM(fold, BF16),
        pltpu.VMEM((n1 - 1, *fold), BF16),
        pltpu.VMEM((n2, *fold), BF16),
        pltpu.VMEM((4 * CH, NCOL), F32),
        pltpu.VMEM((n2 - 1, sm_rows, NCOL), F32),
        pltpu.VMEM((sm_rows, NCOL), F32),
        pltpu.VMEM((n1 - 1, sm_rows, NCOL), F32),
        pltpu.VMEM((n2, sm_rows, NCOL), F32),
        dma((9,)),
        dma((3, 8)),
        dma((3, 8)),
        dma((nr - 1,)),
        dma((nr - 1,)),
        dma((nr - 1,)),
        dma((nr - 1,)),
        dma((nr - 1,)),
        dma((nr - 1,)),
        dma((4,)),
        dma((4,)),
        dma((2,)),
        dma((2,)),
    ]
    results = (
        jax.ShapeDtypeStruct((NT, CO, 128), F32),
        jax.ShapeDtypeStruct((NT * NAT, NCOL), BF16),
        jax.ShapeDtypeStruct((NAT, NCOL), F32),
        jax.ShapeDtypeStruct((3, 3, CH), F32),
        jax.ShapeDtypeStruct((2 * CH, 2 * CH), F32),
        jax.ShapeDtypeStruct((CH, CH), F32),
        jax.ShapeDtypeStruct((CH, CH), F32),
        jax.ShapeDtypeStruct((CO, 16 * CH), F32),
    )
    out = pl.pallas_call(
        functools.partial(kernel, nr, na, scale),
        out_shape=tuple(pltpu.VMEM(x.shape, x.dtype) for x in results),
        in_specs=[hbm] * 7 + [smem] * 2 + [hbm],
        out_specs=(vmem,) * 8,
        scratch_shapes=scratch,
        compiler_params=pltpu.CompilerParams(
            collective_id=0, has_side_effects=True, vmem_limit_bytes=52 * 1024 * 1024
        ),
        name="section",
    )(
        features.reshape(NT * NAT, NCOL),
        state_init.reshape(NAT, NCOL),
        kern.transpose(1, 2, 0),
        gate,
        cand,
        recur,
        down,
        owner_map,
        dest_map,
        cart_cot.reshape(NT, CO, 128),
    )
    cart, gfeat, gstate, gkern, ggate, gcand, grecur, gdown = pl.pallas_call(
        publish,
        out_shape=results,
        in_specs=[vmem] * 8,
        out_specs=(pl.BlockSpec(memory_space=pl.ANY),) * 8,
        scratch_shapes=[dma((8,))],
        compiler_params=pltpu.CompilerParams(vmem_limit_bytes=1024 * 1024),
        name="publish",
    )(*(pltpu.with_memory_space_constraint(x, pltpu.VMEM) for x in out))
    return (
        cart.reshape(1, 1, NT, CO, 128),
        gfeat.reshape(NT, CH, NROW, NCOL),
        gstate.reshape(CH, NROW, NCOL),
        gkern.transpose(2, 0, 1),
        ggate,
        gcand,
        grecur,
        gdown,
    )


def solution(mesh):
    nr, na = mesh.shape["range"], mesh.shape["azimuth"]
    tile = P(None, "range", "azimuth")
    maps = P("range", "azimuth", None)
    cartesian = P("range", "azimuth", None, None, None)
    features = P(None, None, "range", "azimuth")
    return jax.shard_map(
        functools.partial(on_device, nr, na),
        mesh=mesh,
        in_specs=(features, tile, P(), P(), P(), P(), P(), maps, maps, cartesian),
        out_specs=(cartesian, features, tile, P(), P(), P(), P(), P()),
        check_vma=False,
    )
```

```python
import functools
import math

import jax
import jax.numpy as jnp
from jax import lax
from jax.experimental import pallas as pl
from jax.experimental.pallas import tpu as pltpu
from jax.sharding import PartitionSpec as P

MESH = pl.DeviceIdType.MESH
F32 = jnp.float32
BF16 = jnp.bfloat16
I32 = jnp.int32

CH = 64
NT = 4
NROW = 16
NCOL = 128
CELLS = NROW * NCOL
NAT = CH * NROW
CO = 128
SPAN = 512
GROUP = 16


def iota(shape, dim):
    return lax.broadcasted_iota(I32, shape, dim)


def nn(left, right):
    return lax.dot_general(left, right, (((1,), (0,)), ((), ())), preferred_element_type=F32)


def nt(left, right):
    return lax.dot_general(left, right, (((1,), (1,)), ((), ())), preferred_element_type=F32)


def remote(src, dst, send_sem, recv_sem, device):
    return pltpu.make_async_remote_copy(
        src_ref=src,
        dst_ref=dst,
        send_sem=send_sem,
        recv_sem=recv_sem,
        device_id=device,
        device_id_type=MESH,
    )


def kernel(
    nr,
    na,
    scale,
    feat_in,
    state_in,
    kern_in,
    gate_in,
    cand_in,
    recur_in,
    down_in,
    owner,
    dest,
    cot_in,
    cart,
    gfeat,
    gstate,
    gkern,
    ggate,
    gcand,
    grecur,
    gdown,
    feat,
    state,
    kern,
    cand,
    recur,
    down,
    fx,
    xs,
    stk,
    hs,
    s_a,
    s_b,
    s_c,
    s_r,
    s_u,
    flow_in,
    pt,
    hcat,
    perm,
    pick,
    spread,
    wall,
    wall_t,
    wp,
    wb,
    wk,
    dlt,
    dcv,
    carry,
    dwacc,
    gkacc,
    gd,
    row_s,
    row_r,
    col_s,
    col_r,
    cor_s,
    cor_r,
    cot_all,
    key_all,
    blk_all,
    gds,
    gdr,
    gd2,
    gd2r,
    gd3,
    sm1s,
    sm1r,
    sm2,
    sm2r,
    sm3,
    in_sem,
    halo_ss,
    halo_rs,
    cot_ss,
    cot_rs,
    key_ss,
    key_rs,
    blk_ss,
    blk_rs,
    xy_ss,
    xy_rs,
    z_ss,
    z_rs,
):
    r = lax.axis_index("range")
    a = lax.axis_index("azimuth")
    n2 = na // 2
    n1 = nr * 2
    k2 = a // 2
    zl = a % 2
    k1 = r * 2 + zl

    def ring_r(d):
        return lax.rem(r + d + nr, nr)

    def ring_a(d):
        return lax.rem(a + d + na, na)

    def xy_device(d):
        return (r, lax.rem(k2 + d, n2) * 2 + zl)

    def z_device(d):
        m = lax.rem(k1 + d, n1)
        return (m // 2, k2 * 2 + m % 2)

    barrier = pltpu.get_barrier_semaphore()

    def greet(device):
        pl.semaphore_signal(barrier, inc=1, device_id=device, device_id_type=MESH)

    diagonals = [(-1, -1), (-1, 1), (1, -1), (1, 1)]
    for da in (-1, 1):
        greet((r, ring_a(da)))
    for dr, da in diagonals:
        greet((ring_r(dr), ring_a(da)))

    for d in range(1, n2):
        greet(xy_device(d))
    for d in range(1, n1):
        greet(z_device(d))

    fetches = [
        pltpu.make_async_copy(src, dst, in_sem.at[n])
        for n, (src, dst) in enumerate(
            (
                (feat_in.at[pl.ds(0, NAT)], feat.at[pl.ds(0, NAT)]),
                (feat_in.at[pl.ds(NAT, (NT - 1) * NAT)], feat.at[pl.ds(NAT, (NT - 1) * NAT)]),
                (state_in, state),
                (kern_in, kern),
                (gate_in, wall.at[pl.ds(0, 2 * CH)]),
                (cand_in, cand),
                (recur_in, recur),
                (down_in, down),
                (cot_in, cot_all.at[r]),
            )
        )
    ]
    for fetch in fetches:
        fetch.start()

    lane = iota((GROUP, NCOL), 1)
    lane8 = lane // 8
    lane16 = lane // 16

    def chans(g):
        if isinstance(g, int):
            return pl.ds(g * GROUP, GROUP)
        return pl.ds(pl.multiple_of(g * GROUP, GROUP), GROUP)

    def feature_row(t, g, i):
        return fx[pl.ds(t * NAT + g * GROUP * NROW + i, GROUP, stride=NROW), :]

    def dconv_row(t, g, i):
        return dcv[t, chans(g), pl.ds(i * NCOL, NCOL)]

    def pack(ph, batch, slices, row):
        def step(g, c):
            cs = chans(g)
            corner = jnp.zeros((GROUP, NCOL), F32)
            for t in slices:
                left = jnp.zeros((GROUP, NCOL), F32)
                right = jnp.zeros((GROUP, NCOL), F32)
                for i in range(NROW):
                    x = row(t, g, i)
                    y = pltpu.roll(x, 8 * i + 8, 1) if i < NROW - 1 else x
                    right = jnp.where(lane8 == i, y, right)
                    left = jnp.where(lane8 == (i + 1) % 16, y, left)
                    if i == 0:
                        row_s[ph, 0, t, cs, :] = x.astype(BF16)
                        y = pltpu.roll(x, 32 * t + 8, 1)
                        corner = jnp.where(lane16 == 2 * t, y, corner)
                    if i == NROW - 1:
                        row_s[ph, 1, t, cs, :] = x.astype(BF16)
                        y = pltpu.roll(x, (32 * t + 24) % NCOL, 1)
                        corner = jnp.where(lane16 == 2 * t + 1, y, corner)
                col_s[ph, 0, t, cs, :] = pltpu.roll(left, NCOL - 16, 1).astype(BF16)
                col_s[ph, 1, t, cs, :] = right.astype(BF16)
            cor_s[batch, cs, :] = corner.astype(BF16)
            return c

        lax.fori_loop(0, 4, step, 0)

    def halo_copies(ph, batch, first, count):
        copies = []
        some = pl.ds(first, count)
        for end, d in ((0, -1), (1, 1)):
            n = len(copies)
            copies.append(
                remote(
                    row_s.at[ph, end, some],
                    row_r.at[ph, 1 - end, some],
                    halo_ss.at[batch, n],
                    halo_rs.at[batch, n],
                    (ring_r(d), a),
                )
            )
        for end, d in ((0, -1), (1, 1)):
            n = len(copies)
            copies.append(
                remote(
                    col_s.at[ph, end, some],
                    col_r.at[ph, 1 - end, some],
                    halo_ss.at[batch, n],
                    halo_rs.at[batch, n],
                    (r, ring_a(d)),
                )
            )
        for j, (dr, da) in enumerate(diagonals):
            n = len(copies)
            copies.append(
                remote(
                    cor_s.at[batch],
                    cor_r.at[batch, 3 - j],
                    halo_ss.at[batch, n],
                    halo_rs.at[batch, n],
                    (ring_r(dr), ring_a(da)),
                )
            )
        return copies

    has_low = (r > 0).astype(F32)
    has_high = (r < nr - 1).astype(F32)

    def windows(ph, batch, row, t, g):
        cs = chans(g)
        halo_l = col_r[ph, 0, t, cs, :].astype(F32)
        halo_h = col_r[ph, 1, t, cs, :].astype(F32)
        out = [[None] * (NROW + 2) for _ in range(3)]

        def put(pos, x, low, high):
            out[0][pos] = jnp.where(lane < 8, low, pltpu.roll(x, 8, 1))
            out[1][pos] = x
            out[2][pos] = jnp.where(lane >= NCOL - 8, high, pltpu.roll(x, NCOL - 8, 1))

        for i in range(NROW):
            x = row(t, g, i)
            w = pltpu.roll(jnp.where(lane8 == i, halo_l, halo_h), (NCOL - 8 * i) % NCOL, 1)
            put(i + 1, x, w, w)
        for end in (0, 1):
            keep = has_low if end == 0 else has_high
            spot = 2 * t + (1 - end)
            x = row_r[ph, end, t, cs, :].astype(F32) * keep
            c_l = cor_r[batch, 2 * end, cs, :].astype(F32) * keep
            c_h = cor_r[batch, 2 * end + 1, cs, :].astype(F32) * keep
            low = pltpu.roll(c_l, lax.rem(NCOL - 16 * spot, NCOL), 1)
            high = pltpu.roll(c_h, 112 - 16 * spot, 1)
            put(0 if end == 0 else NROW + 1, x, low, high)
        return out

    def convolve(shifted, g, flipped, store):
        cs = chans(g)
        taps = [wk[8 - n if flipped else n, cs, :] for n in range(9)]
        for i in range(NROW):
            total = taps[0] * shifted[0][i]
            for n in range(1, 9):
                total = total + taps[n] * shifted[n % 3][i + n // 3]
            store(i, total)

    def widen(n, c):
        at = pl.ds(pl.multiple_of(n * 256, 256), 256)
        fx[at, :] = feat[at, :].astype(F32)
        return c

    key_row = iota((8, NCOL), 0)
    keys = jnp.zeros((8, NCOL), I32)
    for b in range(NT):
        keys = jnp.where(key_row == b, owner[0, 0, b] * NT + dest[0, 0, b], keys)
    key_all[r] = keys

    fetches[0].wait()
    lax.fori_loop(0, NAT // 256, widen, 0)
    pack(0, 0, [0], feature_row)
    pl.semaphore_wait(barrier, 6 + (n2 - 1) + (n1 - 1))
    first_halo = halo_copies(0, 0, 0, 1)
    for copy in first_halo:
        copy.start()
    fetches[1].wait()
    lax.fori_loop(NAT // 256, NT * NAT // 256, widen, 0)
    pack(0, 1, list(range(1, NT)), feature_row)
    rest_halo = halo_copies(0, 1, 1, NT - 1)
    for copy in rest_halo:
        copy.start()

    cot_copies = []
    key_copies = []
    for d in range(1, nr):
        device = (ring_r(d), a)
        key_copies.append(
            remote(key_all.at[r], key_all.at[r], key_ss.at[d - 1], key_rs.at[d - 1], device)
        )
        cot_copies.append(
            remote(cot_all.at[r], cot_all.at[r], cot_ss.at[d - 1], cot_rs.at[d - 1], device)
        )

    fetches[-1].wait()
    for copy in cot_copies + key_copies:
        copy.start()


    def make_perm(n, c):
        at = pl.multiple_of(n * 128, 128)
        src = iota((128, 1), 0) + at
        to = (src % 4) * 256 + ((src // 4) % 4) * CH + src // 16
        perm[pl.ds(at, 128), :] = (iota((128, 1024), 1) == to).astype(F32).astype(BF16)
        return c

    lax.fori_loop(0, 8, make_perm, 0)

    def make_pick(n, c):
        at = pl.multiple_of(n * 128, 128)
        src = iota((128, 1), 0) + at
        to = (src % 4) * 128 + (src // 128) * 32 + (src % 128) // 4
        pick[pl.ds(at, 128), :] = (iota((128, SPAN), 1) == to).astype(F32).astype(BF16)
        return c

    lax.fori_loop(0, 4, make_pick, 0)
    dst = iota((128, SPAN), 1)
    spread[...] = (iota((128, SPAN), 0) == (dst // 128) * 32 + (dst % 128) // 4).astype(F32).astype(BF16)

    place = iota((CH, 2 * CH), 1) - iota((CH, 2 * CH), 0)
    for fetch in fetches[2:-1]:
        fetch.wait()
    wall[2 * CH : 3 * CH, :] = nn(cand[...], (place == 0).astype(F32).astype(BF16)).astype(BF16)
    wall[3 * CH : 4 * CH, :] = nn(recur[...], (place == CH).astype(F32).astype(BF16)).astype(BF16)
    wall_t[...] = wall[...].astype(F32).T.astype(BF16)
    for q in range(4):
        part = nn(down[...], perm[:, q * 256 : (q + 1) * 256])
        wp[:, q * 256 : (q + 1) * 256] = part.astype(BF16)
        wb[:, q * 128 : (q + 1) * 128] = part.T.astype(BF16)
    for n in range(9):
        line = kern[n // 3, n % 3 : n % 3 + 1, :]
        wk[n] = jnp.broadcast_to(line, (NCOL, CH)).T
    gstate[...] = state[...].astype(F32)
    for i in range(NROW):
        hs[0, :, i * NCOL : (i + 1) * NCOL] = gstate[pl.ds(i, CH, stride=NROW), :]

    def conv_forward(batch, n, c):
        t, g = n // 4, n % 4
        cs = chans(g)
        shifted = windows(0, batch, feature_row, t, g)
        for b in range(3):
            for i in range(NROW + 2):
                xs[t, b, i, cs, :] = shifted[b][i]

        def store(i, total):
            stk[t, cs, i * NCOL : (i + 1) * NCOL] = total.astype(BF16)

        convolve(shifted, g, False, store)
        return c

    def forward(t, c):
        for ic in range(4):
            ls = slice(ic * SPAN, (ic + 1) * SPAN)
            h = hs[t, :, ls]
            stk[t, CH : 2 * CH, ls] = h.astype(BF16)
            pre = nn(wall[...], stk[t, :, ls])
            u = 0.5 * jnp.tanh(0.5 * pre[0:CH]) + 0.5
            z = 0.5 * jnp.tanh(0.5 * pre[CH : 2 * CH]) + 0.5
            rec = pre[3 * CH : 4 * CH]
            act = jnp.tanh(pre[2 * CH : 3 * CH] + z * rec)
            gap = act - h
            step = u * gap
            new = h + step
            hs[t + 1, :, ls] = new
            s_u[t, :, ls] = u
            s_r[t, :, ls] = z
            s_a[t, :, ls] = step * (1.0 - u)
            s_b[t, :, ls] = u * (1.0 - act * act)
            s_c[t, :, ls] = rec * z * (1.0 - z)
            new_bf = new.astype(BF16)
            for p in range(4):
                hcat[p * CH : (p + 1) * CH, ic * NCOL : (ic + 1) * NCOL] = new_bf[
                    :, p * NCOL : (p + 1) * NCOL
                ]
        sorted_lanes = nn(hcat[...], pick[...])
        for q in range(4):
            pt[t, q * 256 : (q + 1) * 256, :] = sorted_lanes[:, q * 128 : (q + 1) * 128].astype(BF16)
        blk_all[r, t] = nn(wp[...], pt[t]).astype(BF16)
        return c

    gd[...] = jnp.zeros(gd.shape, F32)
    sub = iota((CO, SPAN), 1) % 4

    def coarse_back(t, c):
        block = cot_all[owner[0, 0, t], dest[0, 0, t]]
        wide = nn(block, spread[...])
        each = [jnp.where(sub == q, wide, 0.0).astype(BF16) for q in range(4)]
        flow_in[t] = nn(wb[...], jnp.concatenate(each, axis=0))
        gd[...] += nt(block, pt[t])
        return c

    for copy in first_halo:
        copy.wait_recv()
    lax.fori_loop(0, 4, functools.partial(conv_forward, 0), 0)
    forward(0, 0)
    for copy in rest_halo:
        copy.wait_recv()
    lax.fori_loop(4, 4 * NT, functools.partial(conv_forward, 1), 0)
    for t in range(1, NT - 1):
        forward(t, 0)
    for copy in cot_copies:
        copy.wait_recv()
    coarse_back(0, 0)
    forward(NT - 1, 0)
    for t in range(1, NT):
        coarse_back(t, 0)

    blk_copies = []
    for d in range(1, nr):
        device = (ring_r(d), a)
        blk_copies.append(
            remote(blk_all.at[r], blk_all.at[r], blk_ss.at[d - 1], blk_rs.at[d - 1], device)
        )
    for copy in blk_copies:
        copy.start()

    fold_rows, fold_cols = gd2.shape
    own_rows = CO // n2
    parts = fold_rows // own_rows
    sums = gd[...]
    for k in range(n2):
        mine = sums[k * own_rows : (k + 1) * own_rows]
        gds[k * fold_rows : (k + 1) * fold_rows] = jnp.concatenate(
            [mine[:, j * fold_cols : (j + 1) * fold_cols] for j in range(parts)], axis=0
        ).astype(BF16)

    def scatter(slot, src, piece, dst):
        def make(d):
            at = pl.ds(pl.multiple_of(lax.rem(k2 + d, n2) * piece, piece), piece)
            return remote(src.at[at], dst.at[d - 1], xy_ss.at[slot], xy_rs.at[slot], xy_device(d))

        every = remote(dst, dst, xy_ss.at[slot], xy_rs.at[slot], xy_device(1))
        return [make(d) for d in range(1, n2)], every

    def along_z(slot, src, dst):
        def make(d):
            return remote(src, dst.at[d - 1], z_ss.at[slot], z_rs.at[slot], z_device(d))

        every = remote(dst, dst, z_ss.at[slot], z_rs.at[slot], z_device(1))
        return [make(d) for d in range(1, n1)], every

    def gather(slot, buf):
        def make(d):
            return remote(buf.at[k2], buf.at[k2], xy_ss.at[slot], xy_rs.at[slot], xy_device(d))

        rest = buf.at[pl.ds(0, n2 - 1)]
        every = remote(rest, rest, xy_ss.at[slot], xy_rs.at[slot], xy_device(1))
        return [make(d) for d in range(1, n2)], every

    def start_all(exchange):
        for copy in exchange[0]:
            copy.start()

    def wait_all(exchange):
        exchange[1].wait_recv()

    def sent_all(exchange):
        exchange[1].wait_send()

    big1 = scatter(0, gds, fold_rows, gdr)
    big2 = along_z(0, gd2, gd2r)
    big3 = gather(1, gd3)
    sm_rows = 4 * CH // n2
    small1 = scatter(2, sm1s, sm_rows, sm1r)
    small2 = along_z(1, sm2, sm2r)
    small3 = gather(3, sm3)

    def sum_slots(own, buf, count):
        total = own
        for d in range(count):
            total = total + buf[d].astype(F32)
        return total

    start_all(big1)

    def big_second():
        wait_all(big1)
        own = gds[pl.ds(pl.multiple_of(k2 * fold_rows, fold_rows), fold_rows), :]
        gd2[...] = sum_slots(own.astype(F32), gdr, n2 - 1).astype(BF16)
        start_all(big2)

    def big_third():
        wait_all(big2)
        total = sum_slots(gd2[...].astype(F32), gd2r, n1 - 1) * scale
        flat = jnp.concatenate(
            [total[j * own_rows : (j + 1) * own_rows] for j in range(parts)], axis=1
        )
        mine = nt(jnp.concatenate([flat] * parts, axis=0).astype(BF16), perm[...])[0:own_rows]
        gd3[k2] = jnp.concatenate(
            [mine[:, j * fold_cols : (j + 1) * fold_cols] for j in range(parts)], axis=0
        ).astype(BF16)
        start_all(big3)

    carry[...] = jnp.zeros(carry.shape, F32)
    dwacc[...] = jnp.zeros(dwacc.shape, F32)
    gkacc[...] = jnp.zeros(gkacc.shape, F32)

    def backward(n, c):
        t = NT - 1 - n
        for ic in range(4):
            ls = slice(ic * SPAN, (ic + 1) * SPAN)
            rows_in = [
                flow_in[t, p * CH : (p + 1) * CH, ic * NCOL : (ic + 1) * NCOL] for p in range(4)
            ]
            flow = carry[:, ls] + jnp.concatenate(rows_in, axis=1)
            act = flow * s_b[t, :, ls]
            dlt[0:CH, ls] = (flow * s_a[t, :, ls]).astype(BF16)
            dlt[CH : 2 * CH, ls] = (act * s_c[t, :, ls]).astype(BF16)
            dlt[2 * CH : 3 * CH, ls] = act.astype(BF16)
            dlt[3 * CH : 4 * CH, ls] = (act * s_r[t, :, ls]).astype(BF16)
            rev = nn(wall_t[...], dlt[:, ls])
            dcv[t, :, ls] = rev[0:CH].astype(BF16).astype(F32)
            carry[:, ls] = (1.0 - s_u[t, :, ls]) * flow + rev[CH : 2 * CH]
        dwacc[...] += nt(dlt[...], stk[t])

        def kernel_grad(g, c2):
            cs = chans(g)
            grads = [dcv[t, cs, i * NCOL : (i + 1) * NCOL] for i in range(NROW)]
            for tap in range(9):
                total = gkacc[tap, cs, :]
                for i in range(NROW):
                    total = total + grads[i] * xs[t, tap % 3, i + tap // 3, cs, :]
                gkacc[tap, cs, :] = total
            return c2

        for g in range(4):
            kernel_grad(g, 0)
        if n == 3:
            big_second()
        return c

    for n in range(NT):
        backward(n, 0)

    lanes = iota((CH, NCOL), 1)
    sm1s[0 : 2 * CH, :] = dwacc[0 : 2 * CH, :]
    sm1s[2 * CH : 3 * CH, :] = jnp.where(
        lanes < CH, dwacc[2 * CH : 3 * CH, :], dwacc[3 * CH : 4 * CH, :]
    )
    columns = jnp.zeros((CH, NCOL), F32)
    for tap in range(9):
        columns = jnp.where(lanes == tap, jnp.sum(gkacc[tap], axis=1, keepdims=True), columns)
    sm1s[3 * CH : 4 * CH, :] = columns
    start_all(small1)

    pack(1, 2, list(range(NT)), dconv_row)
    halo1 = halo_copies(1, 2, 0, NT)
    for copy in halo1:
        copy.start()

    for i in range(NROW):
        gstate[pl.ds(i, CH, stride=NROW), :] = carry[:, i * NCOL : (i + 1) * NCOL]

    wait_all(small1)
    own = sm1s[pl.ds(pl.multiple_of(k2 * sm_rows, sm_rows), sm_rows), :]
    sm2[...] = sum_slots(own, sm1r, n2 - 1)
    start_all(small2)

    for copy in key_copies + blk_copies:
        copy.wait_recv()

    def gather_blocks(n, c):
        at = pl.ds(pl.multiple_of(n * 32, 32), 32)
        totals = [jnp.zeros((32, NCOL), F32) for _ in range(NT)]
        for src in range(nr):
            for b in range(NT):
                key = key_all[src, b : b + 1, :]
                block = blk_all[src, b, at, :].astype(F32)
                for d in range(NT):
                    totals[d] = totals[d] + jnp.where(key == r * NT + d, block, 0.0)
        for d in range(NT):
            cart[d, at, :] = totals[d]
        return c

    lax.fori_loop(0, 4, gather_blocks, 0)
    big_third()

    wait_all(small2)
    sm3[k2] = sum_slots(sm2[...], sm2r, n1 - 1) * scale
    start_all(small3)

    for copy in halo1:
        copy.wait_recv()

    def conv_backward(n, c):
        t, g = n // 4, n % 4
        shifted = windows(1, 2, dconv_row, t, g)

        def store(i, total):
            fx[pl.ds(t * NAT + g * GROUP * NROW + i, GROUP, stride=NROW), :] = total

        convolve(shifted, g, True, store)
        at = pl.ds(pl.multiple_of(n * 256, 256), 256)
        gfeat[at, :] = fx[at, :].astype(BF16)
        return c

    lax.fori_loop(0, 4 * NT, conv_backward, 0)

    wait_all(big3)
    for k in range(n2):
        mine = gd3[k].astype(F32)
        for j in range(parts):
            gdown[k * own_rows : (k + 1) * own_rows, j * fold_cols : (j + 1) * fold_cols] = mine[
                j * own_rows : (j + 1) * own_rows
            ]

    wait_all(small3)
    small = sm3[...].reshape(4 * CH, NCOL)
    ggate[...] = small[0 : 2 * CH]
    middle = small[2 * CH : 3 * CH]
    gcand[...] = middle[:, 0:CH]
    grecur[...] = pltpu.roll(middle, CH, 1)[:, 0:CH]
    lines = small[3 * CH : 4 * CH].T
    for tap in range(9):
        gkern[tap // 3, tap % 3 : tap % 3 + 1, :] = lines[tap : tap + 1, :]

    for copy in first_halo + rest_halo + halo1 + cot_copies + key_copies + blk_copies:
        copy.wait_send()
    sent_all(big1)
    sent_all(big2)
    sent_all(big3)
    sent_all(small1)
    sent_all(small2)
    sent_all(small3)


def publish(*refs):
    count = (len(refs) - 1) // 2
    copies = [
        pltpu.make_async_copy(refs[n], refs[count + n], refs[-1].at[n]) for n in range(count)
    ]
    for copy in copies:
        copy.start()
    for copy in copies:
        copy.wait()


def on_device(nr, na, *args):
    (features, state_init, kern, gate, cand, recur, down, owner_map, dest_map, cart_cot) = args
    scale = 1.0 / math.sqrt(NT * CELLS * nr * na)
    n2, n1 = na // 2, nr * 2
    own_rows = CO // n2
    parts = max(1, 16 // own_rows)
    fold = (own_rows * parts, 16 * CH // parts)
    sm_rows = 4 * CH // n2
    vmem = pl.BlockSpec(memory_space=pltpu.VMEM)
    smem = pl.BlockSpec(memory_space=pltpu.SMEM)
    hbm = pl.BlockSpec(memory_space=pltpu.HBM)
    dma = pltpu.SemaphoreType.DMA
    cells = (NT, CH, CELLS)
    scratch = [
        pltpu.VMEM((NT * NAT, NCOL), BF16),
        pltpu.VMEM((NAT, NCOL), BF16),
        pltpu.VMEM((3, 3, CH), F32),
        pltpu.VMEM((CH, CH), BF16),
        pltpu.VMEM((CH, CH), BF16),
        pltpu.VMEM((CO, 16 * CH), BF16),
        pltpu.VMEM((NT * NAT, NCOL), F32),
        pltpu.VMEM((NT, 3, NROW + 2, CH, NCOL), F32),
        pltpu.VMEM((NT, 2 * CH, CELLS), BF16),
        pltpu.VMEM((NT + 1, CH, CELLS), F32),
        pltpu.VMEM(cells, F32),
        pltpu.VMEM(cells, F32),
        pltpu.VMEM(cells, F32),
        pltpu.VMEM(cells, F32),
        pltpu.VMEM(cells, F32),
        pltpu.VMEM((NT, 4 * CH, SPAN), F32),
        pltpu.VMEM((NT, 16 * CH, 128), BF16),
        pltpu.VMEM((4 * CH, SPAN), BF16),
        pltpu.VMEM((1024, 1024), BF16),
        pltpu.VMEM((SPAN, SPAN), BF16),
        pltpu.VMEM((128, SPAN), BF16),
        pltpu.VMEM((4 * CH, 2 * CH), BF16),
        pltpu.VMEM((2 * CH, 4 * CH), BF16),
        pltpu.VMEM((CO, 16 * CH), BF16),
        pltpu.VMEM((4 * CH, 4 * CO), BF16),
        pltpu.VMEM((9, CH, NCOL), F32),
        pltpu.VMEM((4 * CH, CELLS), BF16),
        pltpu.VMEM(cells, F32),
        pltpu.VMEM((CH, CELLS), F32),
        pltpu.VMEM((4 * CH, 2 * CH), F32),
        pltpu.VMEM((9, CH, NCOL), F32),
        pltpu.VMEM((CO, 16 * CH), F32),
        pltpu.VMEM((2, 2, NT, CH, NCOL), BF16),
        pltpu.VMEM((2, 2, NT, CH, NCOL), BF16),
        pltpu.VMEM((2, 2, NT, CH, NCOL), BF16),
        pltpu.VMEM((2, 2, NT, CH, NCOL), BF16),
        pltpu.VMEM((3, CH, NCOL), BF16),
        pltpu.VMEM((3, 4, CH, NCOL), BF16),
        pltpu.VMEM((nr, NT, CO, 128), BF16),
        pltpu.VMEM((nr, 8, 128), I32),
        pltpu.VMEM((nr, NT, CO, 128), BF16),
        pltpu.VMEM((n2 * fold[0], fold[1]), BF16),
        pltpu.VMEM((n2 - 1, *fold), BF16),
        pltpu.VMEM(fold, BF16),
        pltpu.VMEM((n1 - 1, *fold), BF16),
        pltpu.VMEM((n2, *fold), BF16),
        pltpu.VMEM((4 * CH, NCOL), F32),
        pltpu.VMEM((n2 - 1, sm_rows, NCOL), F32),
        pltpu.VMEM((sm_rows, NCOL), F32),
        pltpu.VMEM((n1 - 1, sm_rows, NCOL), F32),
        pltpu.VMEM((n2, sm_rows, NCOL), F32),
        dma((9,)),
        dma((3, 8)),
        dma((3, 8)),
        dma((nr - 1,)),
        dma((nr - 1,)),
        dma((nr - 1,)),
        dma((nr - 1,)),
        dma((nr - 1,)),
        dma((nr - 1,)),
        dma((4,)),
        dma((4,)),
        dma((2,)),
        dma((2,)),
    ]
    results = (
        jax.ShapeDtypeStruct((NT, CO, 128), F32),
        jax.ShapeDtypeStruct((NT * NAT, NCOL), BF16),
        jax.ShapeDtypeStruct((NAT, NCOL), F32),
        jax.ShapeDtypeStruct((3, 3, CH), F32),
        jax.ShapeDtypeStruct((2 * CH, 2 * CH), F32),
        jax.ShapeDtypeStruct((CH, CH), F32),
        jax.ShapeDtypeStruct((CH, CH), F32),
        jax.ShapeDtypeStruct((CO, 16 * CH), F32),
    )
    out = pl.pallas_call(
        functools.partial(kernel, nr, na, scale),
        out_shape=tuple(pltpu.VMEM(x.shape, x.dtype) for x in results),
        in_specs=[hbm] * 7 + [smem] * 2 + [hbm],
        out_specs=(vmem,) * 8,
        scratch_shapes=scratch,
        compiler_params=pltpu.CompilerParams(
            collective_id=0, has_side_effects=True, vmem_limit_bytes=52 * 1024 * 1024
        ),
        name="section",
    )(
        features.reshape(NT * NAT, NCOL),
        state_init.reshape(NAT, NCOL),
        kern.transpose(1, 2, 0),
        gate,
        cand,
        recur,
        down,
        owner_map,
        dest_map,
        cart_cot.reshape(NT, CO, 128),
    )
    cart, gfeat, gstate, gkern, ggate, gcand, grecur, gdown = pl.pallas_call(
        publish,
        out_shape=results,
        in_specs=[vmem] * 8,
        out_specs=(pl.BlockSpec(memory_space=pl.ANY),) * 8,
        scratch_shapes=[dma((8,))],
        compiler_params=pltpu.CompilerParams(vmem_limit_bytes=1024 * 1024),
        name="publish",
    )(*(pltpu.with_memory_space_constraint(x, pltpu.VMEM) for x in out))
    return (
        cart.reshape(1, 1, NT, CO, 128),
        gfeat.reshape(NT, CH, NROW, NCOL),
        gstate.reshape(CH, NROW, NCOL),
        gkern.transpose(2, 0, 1),
        ggate,
        gcand,
        grecur,
        gdown,
    )


def solution(mesh):
    nr, na = mesh.shape["range"], mesh.shape["azimuth"]
    tile = P(None, "range", "azimuth")
    maps = P("range", "azimuth", None)
    cartesian = P("range", "azimuth", None, None, None)
    features = P(None, None, "range", "azimuth")
    return jax.shard_map(
        functools.partial(on_device, nr, na),
        mesh=mesh,
        in_specs=(features, tile, P(), P(), P(), P(), P(), maps, maps, cartesian),
        out_specs=(cartesian, features, tile, P(), P(), P(), P(), P()),
        check_vma=False,
    )
```
